512 devices in a mesh: member: 4 (over x), shard: 128 (over y, z, core).
Axes of the slice: x: 4, y: 8, z: 8, core: 2. Of those that a mesh axis runs over, the one named last changes fastest.
Arguments:
- teacher_hidden: bfloat16 [4, 2048, 4096], P('member', 'shard'), may hold values from -80 to 80
- teacher_gain: float32 [4, 4096], P('member'), may hold values from 0.1 to 1.9
- teacher_head: bfloat16 [4, 4096, 65536], P('member', None, 'shard'), may hold values from -0.5 to 0.5
- student_hidden: bfloat16 [2048, 2048], P('shard', 'member'), may hold values from -8 to 8
- student_head: bfloat16 [2048, 65536], P('member', 'shard'), may hold values from -0.6 to 0.6
- positions: int32 [128, 4], P('shard'), may hold values from 0 to 15, as said below
- counts: int32 [128], replicated, may hold values from 1 to 4, 256 in all
- targets: int32 [512], replicated, may hold values from 0 to 65535
Outputs:
- mean_loss: float32 [], replicated
- hidden_grad: bfloat16 [2048, 2048], P('shard', 'member')
The draws below stay inside these ranges and needn't reach their ends.
Inputs may be any that keep to these rules, and one draw needn't show every extreme that they name: Each owner's positions are distinct. The counts sum to exactly 256.
All inputs are finite; a program needn't handle non-finite values.
Results may differ from the reference program's by a relative error of at most 0.0039.
Values may be sent and summed in bfloat16 or wider, within the bound.
No kernel may reach another device: no remote copies, remote signals or barrier semaphores. Data moves between devices by JAX's collectives and lax.ppermute only.
A program may use at most 64 MiB of HBM per device.

```python
import math
import jax
import jax.numpy as jnp
import numpy as np
from jax import lax

DT = 4096
DS = 2048
CAP = 4
WIN = 16
MEMBERS = 4
VOCAB = 65536
ROWS = 512
PACKED = 256
SEQ = 2048
N_SHARD = 128


def planted_columns(key, groups, width, vocab, spread, salt):
    key = jax.random.fold_in(key, salt)
    columns = jax.random.randint(jax.random.fold_in(key, 1), (groups, 3), 0, vocab // 2) * 2
    sign_pattern = jnp.where(jax.random.bernoulli(jax.random.fold_in(key, 2), 0.5, (groups, 3, width)), 1.0, -1.0)
    magnitudes = jax.random.uniform(jax.random.fold_in(key, 3), (groups, 3, width), minval=0.5, maxval=1.5)
    strength = jnp.array([1.0, 1.6, 2.4], jnp.float32)
    vectors = sign_pattern * magnitudes * spread * strength[None, :, None]
    return (columns, sign_pattern, vectors)


def plant_columns(matrix, columns, vectors):
    matrix = matrix.at[:, columns].set(vectors.T)
    return matrix.at[:, columns + 1].set(0.993 * vectors.T)


def draw_teacher_hidden(key, part):
    columns, sign_pattern, vectors = planted_columns(key, MEMBERS, DT, VOCAB, 100.0 / DT, 101)
    key = jax.random.fold_in(key, 11)
    baseline = jax.random.normal(key, (MEMBERS, SEQ, DT), jnp.float32)
    row_scale = jnp.ones((MEMBERS, SEQ, 1), jnp.float32)
    row_ids = jnp.arange(SEQ, dtype=jnp.int32)
    aligned = sign_pattern[:, row_ids % 3, :] * row_scale
    baseline = jnp.where((row_ids % 5 == 0)[None, :, None], aligned, baseline)
    return baseline.astype(jnp.bfloat16)


def draw_teacher_head(key, part):
    columns, sign_pattern, vectors = planted_columns(key, MEMBERS, DT, VOCAB, 100.0 / DT, 101)
    key = jax.random.fold_in(key, 12)
    baseline = 3.0 / math.sqrt(DT) * jax.random.normal(key, (MEMBERS, DT, VOCAB), jnp.float32)
    baseline = jax.vmap(plant_columns)(baseline, columns, vectors)
    return baseline.astype(jnp.bfloat16)


def draw_student_hidden(key, part):
    columns, sign_pattern, vectors = planted_columns(key, 1, DS, VOCAB, 100.0 / DS, 202)
    key = jax.random.fold_in(key, 13)
    baseline = jax.random.normal(key, (SEQ, DS), jnp.float32)
    row_ids = jnp.arange(SEQ, dtype=jnp.int32)
    aligned = sign_pattern[0][row_ids % 3]
    baseline = jnp.where((row_ids % 5 == 0)[:, None], aligned, baseline)
    return baseline.astype(jnp.bfloat16)


def draw_student_head(key, part):
    columns, sign_pattern, vectors = planted_columns(key, 1, DS, VOCAB, 100.0 / DS, 202)
    key = jax.random.fold_in(key, 14)
    baseline = 0.07 * jax.random.normal(key, (DS, VOCAB), jnp.float32)
    baseline = plant_columns(baseline, columns[0], vectors[0])
    return baseline.astype(jnp.bfloat16)


def draw_positions(key, part):
    key = jax.random.fold_in(key, 15)
    scores = jax.random.randint(key, (N_SHARD, WIN), 0, 1 << 20) * WIN + jnp.arange(WIN, dtype=jnp.int32)[None, :]
    scores = scores.at[0, WIN - 1].set(-1)
    scores = scores.at[N_SHARD - 1, 0].set(-1)
    ranking = jnp.argsort(scores, axis=1, stable=True).astype(jnp.int32)
    return ranking[:, :CAP]


def touch_ends(values, stream_key, low, largest):
    dims = values.shape
    place = [jax.random.randint(jax.random.fold_in(stream_key, axis), (), 0, dims[axis]) for axis in range(len(dims))]
    values = values.at[tuple(place)].set(low)
    longest = dims.index(max(dims))
    place[longest] = (place[longest] + 1) % dims[longest]
    return values.at[tuple(place)].set(largest)


def length_profile(count, total, most, skew):
    portions = [(1 << 20) // math.isqrt(standing ** skew) + 1 for standing in range(2, count + 1)]
    rest, given = total - most - (count - 1), [1] * (count - 1)
    while rest > 0:
        candidates = [i for i in range(count - 1) if given[i] < most]
        pool, budget = sum([portions[i] for i in candidates]), rest
        for i in candidates:
            addition = min(most - given[i], max(1, budget * portions[i] // pool), rest)
            given[i] = given[i] + addition
            rest = rest - addition
    return np.array([most] + given)


def uneven_parts(key, number_of, total, limit, slope):
    if number_of == 2:
        one = jax.random.randint(key, (), max(1, total - limit), min(limit, total - 1) + 1)
        return jnp.stack([one, total - one])
    sizes = jnp.asarray(length_profile(number_of, total, limit, slope), jnp.int32)
    twos = (number_of - 1) // 2
    donor, receiver = sizes[1:1 + 2 * twos:2], sizes[2:2 + 2 * twos:2]
    margin = jnp.minimum(donor - 1, limit - receiver)
    moved = jax.random.randint(jax.random.fold_in(key, 1), (twos,), 0, 1 << 20) % (margin + 1)
    sizes = sizes.at[1:1 + 2 * twos:2].set(donor - moved).at[2:2 + 2 * twos:2].set(receiver + moved)
    return sizes[jax.random.permutation(jax.random.fold_in(key, 2), number_of)]


def setup_inputs(seed: int = 0) -> dict:
    arg_keys = jax.random.split(jax.random.key(seed), 9)
    teacher_hidden = draw_teacher_hidden(jax.random.fold_in(arg_keys[8], 71), 0)
    teacher_gain = jnp.clip(1.0 + 0.18 * jax.random.normal(arg_keys[1], (MEMBERS, DT), jnp.float32), 0.1, 1.9)
    teacher_head = draw_teacher_head(jax.random.fold_in(arg_keys[8], 71), 0)
    student_hidden = draw_student_hidden(jax.random.fold_in(arg_keys[8], 71), 0)
    student_head = draw_student_head(jax.random.fold_in(arg_keys[8], 71), 0)
    positions = draw_positions(jax.random.fold_in(arg_keys[8], 71), 0)
    counts = uneven_parts(arg_keys[6], N_SHARD, PACKED, CAP, 2).astype(jnp.int32)
    targets = touch_ends(jax.random.randint(arg_keys[7], (ROWS,), 0, VOCAB), jax.random.fold_in(arg_keys[7], 1), 0, VOCAB - 1).astype(jnp.int32)
    return dict(teacher_hidden=teacher_hidden, teacher_gain=teacher_gain, teacher_head=teacher_head, student_hidden=student_hidden, student_head=student_head, positions=positions, counts=counts, targets=targets)


LOSS_SCALE = 16.0
BLEND = 0.5
EPS = 1e-05

def reference(teacher_hidden, teacher_gain, teacher_head, student_hidden, student_head, positions, counts, targets):
    owners = positions.shape[0]
    row_index = (jnp.arange(owners, dtype=jnp.int32)[:, None] * WIN + positions.astype(jnp.int32)).reshape(-1)
    slot_index = jnp.arange(CAP, dtype=jnp.int32)
    weight = (slot_index[None, :] < counts.astype(jnp.int32)[:, None]).astype(jnp.float32).reshape(-1)

    def teacher_term(running, member_data):
        hidden_rows, gain_row, head_part = member_data
        widened = hidden_rows[row_index].astype(jnp.float32)
        inverse_rms = lax.rsqrt(lax.optimization_barrier(jnp.mean(widened * widened, axis=1, keepdims=True)) + EPS)
        normed = (widened * inverse_rms * gain_row[None, :]).astype(jnp.bfloat16)
        logits = jnp.dot(normed, head_part, preferred_element_type=jnp.float32)
        shifted = jnp.exp(logits - lax.optimization_barrier(jnp.max(logits, axis=1, keepdims=True)))
        return (running + shifted / lax.optimization_barrier(jnp.sum(shifted, axis=1, keepdims=True)), None)
    initial = jnp.zeros((ROWS, VOCAB), jnp.float32)
    running, _ = lax.scan(teacher_term, initial, (teacher_hidden, teacher_gain, teacher_head))
    mean_probs = running / MEMBERS
    picked = student_hidden[row_index]
    logits = jnp.dot(picked, student_head, preferred_element_type=jnp.float32)
    highest = lax.optimization_barrier(jnp.max(logits, axis=1, keepdims=True))
    log_total = highest + jnp.log(lax.optimization_barrier(jnp.sum(jnp.exp(logits - highest), axis=1, keepdims=True)))
    onehot = (jnp.arange(VOCAB, dtype=jnp.int32)[None, :] == targets.astype(jnp.int32)[:, None]).astype(jnp.float32)
    mixture = BLEND * onehot + (1.0 - BLEND) * mean_probs
    row_loss = log_total[:, 0] - lax.optimization_barrier(jnp.sum(mixture * logits, axis=1))
    mean_loss = jnp.sum(weight * row_loss) / jnp.sum(counts).astype(jnp.float32)
    slope_rows = (LOSS_SCALE * weight[:, None] * (jnp.exp(logits - log_total) - mixture)).astype(jnp.bfloat16)
    slot_grad = jnp.dot(slope_rows, student_head.T, preferred_element_type=jnp.float32)
    hidden_grad = jnp.zeros(student_hidden.shape, jnp.float32).at[row_index].set(slot_grad).astype(jnp.bfloat16)
    return (mean_loss, hidden_grad)
```

```python
import jax
import jax.numpy as jnp
from jax import lax
from jax.sharding import Mesh
from jax.sharding import PartitionSpec as P

LOSS_SCALE = 16.0
BLEND = 0.5
EPS = 1e-05
CHIPS = ("y", "z")
OWNERS = ("y", "z", "core")
BF16 = jnp.bfloat16
F32 = jnp.float32


def spread(block, axes, size):
    return lax.all_to_all(
        jnp.broadcast_to(block[None], (size,) + block.shape), axes, 0, 0, tiled=True
    )


def softmax_stats(logits):
    top = jnp.max(logits, axis=1)
    shifted = jnp.exp(logits - top[:, None])
    return top, shifted, jnp.sum(shifted, axis=1)


def global_stats(top, total, owners):
    rows = top.shape[0]
    mine = jnp.concatenate([top, total]).reshape(2 * rows // 128, 128)
    every = spread(mine, OWNERS, owners).reshape(owners, 2 * rows)
    tops, totals = every[:, :rows], every[:, rows:]
    highest = jnp.max(tops, axis=0)
    return highest, jnp.sum(totals * jnp.exp(tops - highest[None, :]), axis=0)


def three_parts(value):
    high = value.astype(BF16)
    rest = value - high.astype(F32)
    middle = rest.astype(BF16)
    low = (rest - middle.astype(F32)).astype(BF16)
    return jnp.stack([high, middle, low])


def on_device(
    teacher_hidden,
    teacher_gain,
    teacher_head,
    student_hidden,
    student_head,
    positions,
    counts,
    targets,
):
    members = lax.axis_size("member")
    chips = lax.axis_size("y") * lax.axis_size("z")
    cores = lax.axis_size("core")
    owners = chips * cores
    member = lax.axis_index("member")
    core = lax.axis_index("core")
    owner = lax.axis_index(OWNERS)
    slot_ids = positions[0]
    cap = slot_ids.shape[0]
    window, width = student_hidden.shape
    vocab = student_head.shape[1]
    padded = owners * cap
    live_rows = padded // 2
    chunk = live_rows // members

    widened = jnp.take(teacher_hidden[0], slot_ids, axis=0).astype(F32)
    inverse_rms = lax.rsqrt(jnp.mean(widened * widened, axis=1, keepdims=True) + EPS)
    normed = (widened * inverse_rms * teacher_gain[0][None, :]).astype(BF16)
    picked = jnp.take(student_hidden, slot_ids, axis=0)
    depth = normed.shape[1]
    both = lax.all_gather(jnp.concatenate([normed, picked], axis=1), "core", axis=0, tiled=True)
    teacher_rows = lax.all_gather(both[:, :depth], CHIPS, axis=0, tiled=True)

    earlier = (
        jnp.arange(owners, dtype=jnp.int32)[:, None] < jnp.arange(owners, dtype=jnp.int32)[None, :]
    )
    starts = jnp.sum(jnp.where(earlier, counts[:, None], 0), axis=0)
    slots = jnp.arange(cap, dtype=jnp.int32)
    places = jnp.where(
        slots[None, :] < counts[:, None], starts[:, None] + slots[None, :], -1
    )
    packed_ids = jnp.arange(live_rows, dtype=jnp.int32)
    pack_mask = packed_ids[:, None] == places.reshape(1, padded)
    pack = pack_mask.astype(BF16)
    live_targets = jnp.sum(jnp.where(pack_mask, targets[None, :], 0), axis=1)

    student_rows = spread(both[:, depth:], CHIPS, chips).reshape(padded, width)
    student_live = jnp.dot(pack, student_rows, preferred_element_type=F32).astype(BF16)
    partial_logits = jnp.dot(student_live, student_head, preferred_element_type=F32)
    student_logits = jnp.sum(
        lax.all_to_all(
            partial_logits.reshape(members, chunk, vocab), "member", 0, 0, tiled=True
        ),
        axis=0,
    )
    top, _, total = softmax_stats(student_logits)
    highest, totals = global_stats(top, total, owners)
    log_total = highest + jnp.log(totals)
    student_probs = jnp.exp(student_logits - log_total[:, None])
    chunk_targets = lax.dynamic_slice_in_dim(live_targets, member * chunk, chunk)
    vocab_ids = owner * vocab + jnp.arange(vocab, dtype=jnp.int32)
    onehot = (vocab_ids[None, :] == chunk_targets[:, None]).astype(F32)

    teacher_live = jnp.dot(pack, teacher_rows, preferred_element_type=F32).astype(BF16)
    teacher_logits = jnp.dot(teacher_live, teacher_head[0], preferred_element_type=F32)
    top, shifted, total = softmax_stats(teacher_logits)
    highest, totals = global_stats(top, total, owners)
    factor = jnp.exp(top - highest) / totals
    teacher_probs = (shifted * factor[:, None]).astype(BF16)
    mean_probs = (
        jnp.sum(
            lax.all_to_all(
                teacher_probs.reshape(members, chunk, vocab), "member", 0, 0, tiled=True
            ).astype(F32),
            axis=0,
        )
        / members
    )
    mixture = BLEND * onehot + (1.0 - BLEND) * mean_probs
    loss = jnp.where(owner == 0, jnp.sum(log_total), 0.0) - jnp.sum(mixture * student_logits)
    slope = (LOSS_SCALE * (student_probs - mixture)).astype(BF16)
    tail = jnp.zeros((16, vocab), BF16)
    tail = lax.dynamic_update_slice(tail, three_parts(loss)[None, :], (0, 0))
    slopes = spread(jnp.concatenate([slope, tail], axis=0), "member", members)
    shard_loss = jnp.sum(slopes[:, chunk, :3].astype(F32))
    slope_live = slopes[:, :chunk].reshape(live_rows, vocab)

    halves = 2
    half = width // halves

    def term(which_core):
        chosen = jnp.take(places.reshape(chips, cores, cap), which_core, axis=1)
        result = 0.0
        for part in range(halves):
            here = jnp.arange(halves, dtype=jnp.int32)[None, :, None] == part
            at = jnp.where(here, chosen[:, None, :], -1).reshape(chips * halves * cap, 1)
            unpack = (at == packed_ids[None, :]).astype(BF16)
            rows = jnp.dot(unpack, slope_live, preferred_element_type=F32).astype(BF16)
            result = result + lax.dot_general(
                rows,
                student_head[part * half : (part + 1) * half],
                (((1,), (1,)), ((), ())),
                preferred_element_type=F32,
            )
        return result

    swap = [(0, 1), (1, 0)]
    arrived = lax.ppermute(term(1 - core), "core", swap)
    other_loss = lax.ppermute(jnp.full((8, 128), shard_loss, F32), "core", swap)
    grads = (term(core) + arrived).reshape(chips, halves * cap, half)
    chip_loss = jnp.broadcast_to((shard_loss + other_loss[0, 0])[None, None, None], (chips, 8, half))
    owned = jnp.sum(
        lax.all_to_all(
            jnp.concatenate([grads, chip_loss], axis=1), CHIPS, 0, 0, tiled=True
        ),
        axis=0,
    )
    mean_loss = owned[halves * cap, 0] / jnp.sum(counts).astype(F32)
    slot_grad = jnp.concatenate(
        [owned[part * cap : (part + 1) * cap] for part in range(halves)], axis=1
    )
    live_here = slots < lax.dynamic_index_in_dim(counts, owner, keepdims=False)
    placed = (
        (jnp.arange(window, dtype=jnp.int32)[:, None] == slot_ids[None, :]) & live_here[None, :]
    ).astype(F32)
    hidden_grad = jnp.sum(placed[:, :, None] * slot_grad[None, :, :], axis=1).astype(BF16)
    return (mean_loss, hidden_grad)


def solution(mesh):
    fine = Mesh(mesh.devices.reshape(4, 8, 8, 2), ("member", "y", "z", "core"))
    placed = (
        P("member", OWNERS, None),
        P("member", None),
        P("member", None, OWNERS),
        P(OWNERS, "member"),
        P("member", OWNERS),
        P(OWNERS, None),
        P(),
        P(),
    )
    return jax.shard_map(
        on_device,
        mesh=fine,
        in_specs=placed,
        out_specs=(P(), P(OWNERS, "member")),
        check_vma=False,
    )
```

```python
import jax
import jax.numpy as jnp
from jax import lax
from jax.sharding import Mesh
from jax.sharding import PartitionSpec as P

LOSS_SCALE = 16.0
BLEND = 0.5
EPS = 1e-05
CHIPS = ("y", "z")
OWNERS = ("y", "z", "core")
BF16 = jnp.bfloat16
F32 = jnp.float32


def spread(block, axes, size):
    return lax.all_to_all(
        jnp.broadcast_to(block[None], (size,) + block.shape), axes, 0, 0, tiled=True
    )


def softmax_stats(logits):
    top = jnp.max(logits, axis=1)
    shifted = jnp.exp(logits - top[:, None])
    return top, shifted, jnp.sum(shifted, axis=1)


def row_stats(*columns):
    flat = jnp.concatenate(columns)
    return flat.reshape(-1, 128)


def on_device(
    teacher_hidden,
    teacher_gain,
    teacher_head,
    student_hidden,
    student_head,
    positions,
    counts,
    targets,
):
    members = lax.axis_size("member")
    ring = lax.axis_size("z")
    chips = lax.axis_size("y") * ring
    cores = lax.axis_size("core")
    owners = chips * cores
    member = lax.axis_index("member")
    core = lax.axis_index("core")
    owner = lax.axis_index(OWNERS)
    slot_ids = positions[0]
    cap = slot_ids.shape[0]
    window, width = student_hidden.shape
    vocab = student_head.shape[1]
    padded = owners * cap
    live_rows = padded // 2
    chunk = live_rows // members
    swap = [(0, 1), (1, 0)]

    widened = jnp.take(teacher_hidden[0], slot_ids, axis=0).astype(F32)
    inverse_rms = lax.rsqrt(jnp.mean(widened * widened, axis=1, keepdims=True) + EPS)
    normed = (widened * inverse_rms * teacher_gain[0][None, :]).astype(BF16)
    depth = normed.shape[1]
    quarter = depth // (2 * cores)
    units = normed.reshape(cap, cores, 2, quarter).transpose(1, 2, 0, 3).reshape(
        1, cores, 2 * cap, quarter
    )
    sent = jnp.broadcast_to(units, (ring,) + units.shape[1:]).reshape(-1, 2 * cap, quarter)
    group_rows = lax.all_to_all(sent, ("z", "core"), 0, 0, tiled=True).reshape(-1, quarter)
    teacher_rows = lax.all_gather(group_rows, "y", axis=0, tiled=True)

    before = (
        jnp.arange(owners, dtype=jnp.int32)[:, None] < jnp.arange(owners, dtype=jnp.int32)[None, :]
    )
    starts = jnp.sum(jnp.where(before, counts[:, None], 0), axis=0)
    slots = jnp.arange(cap, dtype=jnp.int32)
    places = jnp.where(slots[None, :] < counts[:, None], starts[:, None] + slots[None, :], -1)
    packed_ids = jnp.arange(live_rows, dtype=jnp.int32)
    sides = jnp.arange(2, dtype=jnp.int32)
    pack = [
        (
            packed_ids[:, None]
            == jnp.where(sides[None, :, None] == side, places[:, None, :], -1).reshape(1, -1)
        ).astype(BF16)
        for side in range(2)
    ]
    live_targets = jnp.sum(
        jnp.where(packed_ids[:, None] == places.reshape(1, padded), targets[None, :], 0), axis=1
    )

    def packed(rows):
        return jnp.concatenate(
            [jnp.dot(one, rows, preferred_element_type=F32).astype(BF16) for one in pack], axis=1
        )

    picked = jnp.take(student_hidden, slot_ids, axis=0)
    picked = picked.reshape(cap, 2, width // 2).transpose(1, 0, 2).reshape(2 * cap, width // 2)
    student_rows = spread(picked, OWNERS, owners).reshape(-1, width // 2)
    partial_logits = jnp.dot(packed(student_rows), student_head, preferred_element_type=F32)
    logits_chunk = jnp.sum(
        lax.all_to_all(
            partial_logits.reshape(members, chunk, vocab), "member", 0, 0, tiled=True
        ),
        axis=0,
    )
    student_logits = spread(logits_chunk, "member", members).reshape(live_rows, vocab)
    top, _, total = softmax_stats(logits_chunk)
    vocab_ids = owner * vocab + jnp.arange(vocab, dtype=jnp.int32)
    hit = vocab_ids[None, :] == live_targets[:, None]
    hit_chunk = vocab_ids[None, :] == lax.dynamic_slice_in_dim(
        live_targets, member * chunk, chunk
    )[:, None]
    target_part = jnp.sum(jnp.where(hit_chunk, logits_chunk, 0.0), axis=1)
    every = spread(
        row_stats(top, total, target_part, jnp.zeros_like(top)), OWNERS, owners
    ).reshape(owners, 4 * chunk)
    tops = every[:, :chunk]
    highest = jnp.max(tops, axis=0)
    totals = jnp.sum(every[:, chunk : 2 * chunk] * jnp.exp(tops - highest[None, :]), axis=0)
    log_chunk = highest + jnp.log(totals)
    student_loss = jnp.sum(log_chunk) - BLEND * jnp.sum(every[:, 2 * chunk : 3 * chunk])
    log_total = spread(jnp.pad(log_chunk[None, :], ((0, 7), (0, 128 - chunk))), "member", members)
    log_total = log_total[:, 0, :chunk].reshape(live_rows)
    student_slope = jnp.exp(student_logits - log_total[:, None]) - BLEND * hit.astype(F32)

    teacher_rows, student_logits = lax.optimization_barrier((teacher_rows, student_logits))
    mine = packed(teacher_rows)
    other = lax.ppermute(mine, "core", swap)
    own_half = lax.dynamic_slice_in_dim(teacher_head[0], core * (depth // 2), depth // 2, axis=0)
    other_half = lax.dynamic_slice_in_dim(
        teacher_head[0], (1 - core) * (depth // 2), depth // 2, axis=0
    )
    teacher_logits = jnp.dot(mine, own_half, preferred_element_type=F32) + jnp.dot(
        other, other_half, preferred_element_type=F32
    )
    top, shifted, total = softmax_stats(teacher_logits)
    cross = jnp.sum(shifted * student_logits, axis=1)
    every = spread(row_stats(top, total, cross), OWNERS, owners).reshape(owners, 3 * live_rows)
    tops = every[:, :live_rows]
    highest = jnp.max(tops, axis=0)
    scales = jnp.exp(tops - highest[None, :])
    totals = jnp.sum(every[:, live_rows : 2 * live_rows] * scales, axis=0)
    crosses = jnp.sum(every[:, 2 * live_rows :] * scales, axis=0)
    teacher_probs = (shifted * (jnp.exp(top - highest) / totals)[:, None]).astype(BF16)
    loss = student_loss - (1.0 - BLEND) / members * jnp.sum(crosses / totals)

    probs = teacher_probs.astype(F32)
    for step in range(1, members):
        shift = [(i, (i + step) % members) for i in range(members)]
        probs = probs + lax.ppermute(teacher_probs, "member", shift).astype(F32)
    slope = (LOSS_SCALE * (student_slope - (1.0 - BLEND) / members * probs)).astype(BF16)

    half = width // 2

    def term(which_core):
        chosen = jnp.take(places.reshape(chips, cores, cap), which_core, axis=1)
        result = 0.0
        for side in range(2):
            at = jnp.where(sides[None, :, None] == side, chosen[:, None, :], -1).reshape(-1, 1)
            unpack = (at == packed_ids[None, :]).astype(BF16)
            rows = jnp.dot(unpack, slope, preferred_element_type=F32).astype(BF16)
            result = result + lax.dot_general(
                rows,
                student_head[side * half : (side + 1) * half],
                (((1,), (1,)), ((), ())),
                preferred_element_type=F32,
            )
        return result

    arrived = lax.ppermute(term(1 - core), "core", swap)
    grads = (term(core) + arrived).reshape(chips, 2 * cap, half)
    owned = jnp.sum(lax.all_to_all(grads, CHIPS, 0, 0, tiled=True), axis=0)
    losses = spread(jnp.full((8, 128), loss, F32), "member", members)
    mean_loss = jnp.sum(losses[:, 0, 0]) / jnp.sum(counts).astype(F32)
    slot_grad = jnp.concatenate([owned[:cap], owned[cap:]], axis=1)
    live_here = slots < lax.dynamic_index_in_dim(counts, owner, keepdims=False)
    placed = (
        (jnp.arange(window, dtype=jnp.int32)[:, None] == slot_ids[None, :]) & live_here[None, :]
    ).astype(F32)
    hidden_grad = jnp.sum(placed[:, :, None] * slot_grad[None, :, :], axis=1).astype(BF16)
    return (mean_loss, hidden_grad)


def solution(mesh):
    fine = Mesh(mesh.devices.reshape(4, 8, 8, 2), ("member", "y", "z", "core"))
    placed = (
        P("member", OWNERS, None),
        P("member", None),
        P("member", None, OWNERS),
        P(OWNERS, "member"),
        P("member", OWNERS),
        P(OWNERS, None),
        P(),
        P(),
    )
    return jax.shard_map(
        on_device,
        mesh=fine,
        in_specs=placed,
        out_specs=(P(), P(OWNERS, "member")),
        check_vma=False,
    )
```

```python
import jax
import jax.numpy as jnp
from jax import lax
from jax.experimental import pallas as pl
from jax.experimental.pallas import tpu as pltpu
from jax.sharding import Mesh
from jax.sharding import PartitionSpec as P

LOSS_SCALE = 16.0
BLEND = 0.5
EPS = 1e-05
CHIPS = ("y", "z")
OWNERS = ("y", "z", "core")
BF16 = jnp.bfloat16
F32 = jnp.float32


def spread(block, axes, size):
    return lax.all_to_all(
        jnp.broadcast_to(block[None], (size,) + block.shape), axes, 0, 0, tiled=True
    )


def own_rows_kernel(copies, ids_ref, teacher_ref, gain_ref, student_ref, sent_ref):
    cap = ids_ref.shape[1]
    window, depth = teacher_ref.shape[1:]
    width = student_ref.shape[1]
    rows = 4 * cap
    row = lax.broadcasted_iota(jnp.int32, (rows, window), 0) % cap
    column = lax.broadcasted_iota(jnp.int32, (rows, window), 1)
    wanted = jnp.zeros((rows, window), jnp.int32)
    for slot in range(cap):
        wanted = jnp.where(row == slot, ids_ref[0, slot], wanted)
    select = (column == wanted).astype(BF16)
    picked = jnp.dot(select, teacher_ref[0], preferred_element_type=F32)
    inverse_rms = lax.rsqrt(jnp.mean(picked * picked, axis=1, keepdims=True) + EPS)
    normed = picked * inverse_rms * gain_ref[...]
    student = jnp.dot(select, student_ref[...], preferred_element_type=F32)

    def quarters(values):
        part = values.shape[1] // 4
        group = lax.broadcasted_iota(jnp.int32, (rows, part), 0) // cap
        result = values[:, :part]
        for index in range(1, 4):
            result = jnp.where(group == index, values[:, index * part : (index + 1) * part], result)
        return result.astype(BF16)

    teacher_part, student_part = quarters(normed), quarters(student)
    for copy in range(copies):
        sent_ref[copy * rows : (copy + 1) * rows, : depth // 4] = teacher_part
        sent_ref[copy * rows : (copy + 1) * rows, depth // 4 :] = student_part


def own_rows(copies, slot_ids, teacher_hidden, teacher_gain, student_hidden):
    cap = slot_ids.shape[1]
    features = teacher_hidden.shape[2] // 4 + student_hidden.shape[1] // 4
    return pl.pallas_call(
        lambda *refs: own_rows_kernel(copies, *refs),
        out_shape=jax.ShapeDtypeStruct((copies * 4 * cap, features), BF16),
        in_specs=[pl.BlockSpec(memory_space=pltpu.SMEM)]
        + [pl.BlockSpec(memory_space=pltpu.VMEM)] * 3,
        out_specs=pl.BlockSpec(memory_space=pltpu.VMEM),
        name="own_rows",
    )(slot_ids, teacher_hidden, teacher_gain, student_hidden)


def pack_kernel(places_ref, rows_ref, packed_ref, one_ref):
    live = packed_ref.shape[1]

    @pl.when(pl.program_id(0) == 0)
    def _():
        ids = lax.broadcasted_iota(jnp.int32, (live, places_ref.shape[1]), 0)
        for side in range(2):
            one_ref[side] = (ids == places_ref[side : side + 1, :]).astype(BF16)

    for side in range(2):
        packed_ref[side] = jnp.dot(
            one_ref[side], rows_ref[...], preferred_element_type=F32
        ).astype(BF16)


def pack_rows(places, rows, live, parts):
    total, features = rows.shape
    part = features // parts
    return pl.pallas_call(
        pack_kernel,
        grid=(parts,),
        out_shape=jax.ShapeDtypeStruct((2, live, features), BF16),
        in_specs=[
            pl.BlockSpec((2, total), lambda i: (0, 0)),
            pl.BlockSpec((total, part), lambda i: (0, i)),
        ],
        out_specs=pl.BlockSpec((2, live, part), lambda i: (0, 0, i)),
        scratch_shapes=[pltpu.VMEM((2, live, total), BF16)],
        name="pack_rows",
    )(places, rows)


def softmax_stats(logits):
    top = jnp.max(logits, axis=1)
    shifted = jnp.exp(logits - top[:, None])
    return top, shifted, jnp.sum(shifted, axis=1)


def row_stats(*columns):
    flat = jnp.concatenate(columns)
    return flat.reshape(-1, 128)


def on_device(
    teacher_hidden,
    teacher_gain,
    teacher_head,
    student_hidden,
    student_head,
    positions,
    counts,
    targets,
):
    members = lax.axis_size("member")
    ring = lax.axis_size("z")
    chips = lax.axis_size("y") * ring
    cores = lax.axis_size("core")
    owners = chips * cores
    member = lax.axis_index("member")
    core = lax.axis_index("core")
    owner = lax.axis_index(OWNERS)
    slot_ids = positions[0]
    cap = slot_ids.shape[0]
    window, width = student_hidden.shape
    vocab = student_head.shape[1]
    padded = owners * cap
    live_rows = padded // 2
    chunk = live_rows // members
    swap = [(0, 1), (1, 0)]

    sent = own_rows(ring, positions, teacher_hidden, teacher_gain, student_hidden)
    depth = teacher_hidden.shape[2]
    quarter = depth // (2 * cores)
    sent = sent.reshape(ring * cores, 2 * cap, -1)
    group_rows = lax.all_to_all(sent, ("z", "core"), 0, 0, tiled=True)
    group_rows = group_rows.reshape(ring * cores * 2 * cap, -1)
    teacher_rows = lax.all_gather(group_rows[:, :quarter], "y", axis=0, tiled=True)

    before = (
        jnp.arange(owners, dtype=jnp.int32)[:, None] < jnp.arange(owners, dtype=jnp.int32)[None, :]
    )
    starts = jnp.sum(jnp.where(before, counts[:, None], 0), axis=0)
    slots = jnp.arange(cap, dtype=jnp.int32)
    places = jnp.where(slots[None, :] < counts[:, None], starts[:, None] + slots[None, :], -1)
    packed_ids = jnp.arange(live_rows, dtype=jnp.int32)
    sides = jnp.arange(2, dtype=jnp.int32)
    side_places = jnp.stack(
        [
            jnp.where(sides[None, :, None] == side, places[:, None, :], -1).reshape(-1)
            for side in range(2)
        ]
    )
    live_targets = jnp.sum(
        jnp.where(packed_ids[:, None] == places.reshape(1, padded), targets[None, :], 0), axis=1
    )

    def both_halves(mine, other, weights):
        half = weights.shape[0] // cores
        part = half // 2
        result = 0.0
        for values, first in ((mine, core * half), (other, (1 - core) * half)):
            for side in range(2):
                result = result + jnp.dot(
                    values[side],
                    lax.dynamic_slice_in_dim(weights, first + side * part, part, axis=0),
                    preferred_element_type=F32,
                )
        return result

    student_rows = spread(group_rows[:, quarter:], "y", lax.axis_size("y"))
    student_rows = student_rows.reshape(2 * padded, -1)
    mine = pack_rows(side_places, student_rows, live_rows, 1)
    partial_logits = both_halves(mine, lax.ppermute(mine, "core", swap), student_head)
    logits_chunk = jnp.sum(
        lax.all_to_all(
            partial_logits.reshape(members, chunk, vocab), "member", 0, 0, tiled=True
        ),
        axis=0,
    )
    student_logits = spread(logits_chunk, "member", members).reshape(live_rows, vocab)
    top, _, total = softmax_stats(logits_chunk)
    vocab_ids = owner * vocab + jnp.arange(vocab, dtype=jnp.int32)
    hit = vocab_ids[None, :] == live_targets[:, None]
    hit_chunk = vocab_ids[None, :] == lax.dynamic_slice_in_dim(
        live_targets, member * chunk, chunk
    )[:, None]
    target_part = jnp.sum(jnp.where(hit_chunk, logits_chunk, 0.0), axis=1)
    every = spread(
        row_stats(top, total, target_part, jnp.zeros_like(top)), OWNERS, owners
    ).reshape(owners, 4 * chunk)
    tops = every[:, :chunk]
    highest = jnp.max(tops, axis=0)
    totals = jnp.sum(every[:, chunk : 2 * chunk] * jnp.exp(tops - highest[None, :]), axis=0)
    log_chunk = highest + jnp.log(totals)
    student_loss = jnp.sum(log_chunk) - BLEND * jnp.sum(every[:, 2 * chunk : 3 * chunk])

    teacher_rows, student_logits, log_chunk = lax.optimization_barrier(
        (teacher_rows, student_logits, log_chunk)
    )
    mine = pack_rows(side_places, teacher_rows, live_rows, 4)
    teacher_logits = both_halves(mine, lax.ppermute(mine, "core", swap), teacher_head[0])
    top, shifted, total = softmax_stats(teacher_logits)
    cross = jnp.sum(shifted * student_logits, axis=1)
    shifted = shifted.astype(BF16)
    arrived = [shifted] + [
        lax.ppermute(shifted, "member", [(i, (i + step) % members) for i in range(members)])
        for step in range(1, members)
    ]
    every = spread(jnp.concatenate([top, total, cross])[None], OWNERS, owners)
    every = every.reshape(owners, 3 * live_rows)
    tops = every[:, :live_rows]
    highest = jnp.max(tops, axis=0)
    scales = jnp.exp(tops - highest[None, :])
    totals = jnp.sum(every[:, live_rows : 2 * live_rows] * scales, axis=0)
    crosses = jnp.sum(every[:, 2 * live_rows :] * scales, axis=0)
    factor = jnp.exp(top - highest) / totals
    loss = student_loss - (1.0 - BLEND) / members * jnp.sum(crosses / totals)
    factors = spread(
        jnp.concatenate([factor, log_chunk, jnp.full((128 - chunk,), loss)]).reshape(-1, 128), "member", members
    )
    mean_loss = jnp.sum(factors[:, -1, chunk]) / jnp.sum(counts).astype(F32)
    log_total = factors[:, -1, :chunk].reshape(live_rows)
    factors = factors[:, :-1].reshape(members, live_rows)
    ranks = jnp.arange(members, dtype=jnp.int32)[:, None]
    probs = 0.0
    for step in range(members):
        source = (member - step) % members
        scale = jnp.sum(jnp.where(ranks == source, factors, 0.0), axis=0)
        probs = probs + arrived[step].astype(F32) * scale[:, None]
    student_slope = jnp.exp(student_logits - log_total[:, None]) - BLEND * hit.astype(F32)
    slope = (LOSS_SCALE * (student_slope - (1.0 - BLEND) / members * probs)).astype(BF16)

    half = width // 2

    def term(which_core):
        chosen = jnp.take(places.reshape(chips, cores, cap), which_core, axis=1)
        result = 0.0
        for side in range(2):
            at = jnp.where(sides[None, :, None] == side, chosen[:, None, :], -1).reshape(-1, 1)
            unpack = (at == packed_ids[None, :]).astype(BF16)
            rows = jnp.dot(unpack, slope, preferred_element_type=F32).astype(BF16)
            result = result + lax.dot_general(
                rows,
                student_head[side * half : (side + 1) * half],
                (((1,), (1,)), ((), ())),
                preferred_element_type=F32,
            )
        return result

    arrived = lax.ppermute(term(1 - core), "core", swap)
    grads = (term(core) + arrived).reshape(chips, 2 * cap, half)
    owned = jnp.sum(lax.all_to_all(grads, CHIPS, 0, 0, tiled=True), axis=0)
    slot_grad = jnp.concatenate([owned[:cap], owned[cap:]], axis=1)
    live_here = slots < lax.dynamic_index_in_dim(counts, owner, keepdims=False)
    placed = (
        (jnp.arange(window, dtype=jnp.int32)[:, None] == slot_ids[None, :]) & live_here[None, :]
    ).astype(F32)
    hidden_grad = jnp.sum(placed[:, :, None] * slot_grad[None, :, :], axis=1).astype(BF16)
    return (mean_loss, hidden_grad)


def solution(mesh):
    fine = Mesh(mesh.devices.reshape(4, 8, 8, 2), ("member", "y", "z", "core"))
    placed = (
        P("member", OWNERS, None),
        P("member", None),
        P("member", None, OWNERS),
        P(OWNERS, "member"),
        P("member", OWNERS),
        P(OWNERS, None),
        P(),
        P(),
    )
    return jax.shard_map(
        on_device,
        mesh=fine,
        in_specs=placed,
        out_specs=(P(), P(OWNERS, "member")),
        check_vma=False,
    )
```

```python
import jax
import jax.numpy as jnp
from jax import lax
from jax.experimental import pallas as pl
from jax.experimental.pallas import tpu as pltpu
from jax.sharding import Mesh
from jax.sharding import PartitionSpec as P

LOSS_SCALE = 16.0
BLEND = 0.5
EPS = 1e-05
CHIPS = ("y", "z")
OWNERS = ("y", "z", "core")
BF16 = jnp.bfloat16
F32 = jnp.float32


def spread(block, axes, size):
    return lax.all_to_all(
        jnp.broadcast_to(block[None], (size,) + block.shape), axes, 0, 0, tiled=True
    )


def own_rows_kernel(copies, ids_ref, teacher_ref, gain_ref, student_ref, sent_ref):
    cap = ids_ref.shape[1]
    window, depth = teacher_ref.shape[1:]
    width = student_ref.shape[1]
    rows = 4 * cap
    row = lax.broadcasted_iota(jnp.int32, (rows, window), 0) % cap
    column = lax.broadcasted_iota(jnp.int32, (rows, window), 1)
    wanted = jnp.zeros((rows, window), jnp.int32)
    for slot in range(cap):
        wanted = jnp.where(row == slot, ids_ref[0, slot], wanted)
    select = (column == wanted).astype(BF16)
    picked = jnp.dot(select, teacher_ref[0], preferred_element_type=F32)
    inverse_rms = lax.rsqrt(jnp.mean(picked * picked, axis=1, keepdims=True) + EPS)
    normed = picked * inverse_rms * gain_ref[...]
    student = jnp.dot(select, student_ref[...], preferred_element_type=F32)

    def quarters(values):
        part = values.shape[1] // 4
        group = lax.broadcasted_iota(jnp.int32, (rows, part), 0) // cap
        result = values[:, :part]
        for index in range(1, 4):
            result = jnp.where(group == index, values[:, index * part : (index + 1) * part], result)
        return result.astype(BF16)

    teacher_part, student_part = quarters(normed), quarters(student)
    for copy in range(copies):
        sent_ref[copy * rows : (copy + 1) * rows, : depth // 4] = teacher_part
        sent_ref[copy * rows : (copy + 1) * rows, depth // 4 :] = student_part


def own_rows(copies, slot_ids, teacher_hidden, teacher_gain, student_hidden):
    cap = slot_ids.shape[1]
    features = teacher_hidden.shape[2] // 4 + student_hidden.shape[1] // 4
    return pl.pallas_call(
        lambda *refs: own_rows_kernel(copies, *refs),
        out_shape=jax.ShapeDtypeStruct((copies * 4 * cap, features), BF16),
        in_specs=[pl.BlockSpec(memory_space=pltpu.SMEM)]
        + [pl.BlockSpec(memory_space=pltpu.VMEM)] * 3,
        out_specs=pl.BlockSpec(memory_space=pltpu.VMEM),
        name="own_rows",
    )(slot_ids, teacher_hidden, teacher_gain, student_hidden)


def one_hot_kernel(places_ref, rows_ref, packed_ref, one_ref):
    live = packed_ref.shape[1]
    ids = lax.broadcasted_iota(jnp.int32, (live, places_ref.shape[1]), 0)
    for side in range(2):
        one_ref[side] = (ids == places_ref[side : side + 1, :]).astype(BF16)
        packed_ref[side] = jnp.dot(
            one_ref[side], rows_ref[...], preferred_element_type=F32
        ).astype(BF16)


def pack_with_places(places, rows, live):
    total, features = rows.shape
    return pl.pallas_call(
        one_hot_kernel,
        out_shape=(
            jax.ShapeDtypeStruct((2, live, features), BF16),
            jax.ShapeDtypeStruct((2, live, total), BF16),
        ),
        name="pack_student",
    )(places, rows)


def pack_kernel(one_ref, rows_ref, packed_ref):
    for side in range(2):
        packed_ref[side] = jnp.dot(
            one_ref[side], rows_ref[...], preferred_element_type=F32
        ).astype(BF16)


def pack_rows(one, rows, parts):
    total, features = rows.shape
    live = one.shape[1]
    part = features // parts
    return pl.pallas_call(
        pack_kernel,
        grid=(parts,),
        out_shape=jax.ShapeDtypeStruct((2, live, features), BF16),
        in_specs=[
            pl.BlockSpec((2, live, total), lambda i: (0, 0, 0)),
            pl.BlockSpec((total, part), lambda i: (0, i)),
        ],
        out_specs=pl.BlockSpec((2, live, part), lambda i: (0, 0, i)),
        name="pack_teacher",
    )(one, rows)


def softmax_stats(logits):
    top = jnp.max(logits, axis=1)
    shifted = jnp.exp(logits - top[:, None])
    return top, shifted, jnp.sum(shifted, axis=1)


def on_device(
    teacher_hidden,
    teacher_gain,
    teacher_head,
    student_hidden,
    student_head,
    positions,
    counts,
    targets,
):
    members = lax.axis_size("member")
    ring = lax.axis_size("z")
    chips = lax.axis_size("y") * ring
    cores = lax.axis_size("core")
    owners = chips * cores
    member = lax.axis_index("member")
    core = lax.axis_index("core")
    owner = lax.axis_index(OWNERS)
    slot_ids = positions[0]
    cap = slot_ids.shape[0]
    window, width = student_hidden.shape
    vocab = student_head.shape[1]
    padded = owners * cap
    live_rows = padded // 2
    chunk = live_rows // members
    swap = [(0, 1), (1, 0)]

    sent = own_rows(ring, positions, teacher_hidden, teacher_gain, student_hidden)
    depth = teacher_hidden.shape[2]
    quarter = depth // (2 * cores)
    sent = sent.reshape(ring * cores, 2 * cap, -1)
    group_rows = lax.all_to_all(sent, ("z", "core"), 0, 0, tiled=True)
    group_rows = group_rows.reshape(ring * cores * 2 * cap, -1)
    teacher_rows = lax.all_gather(group_rows[:, :quarter], "y", axis=0, tiled=True)

    before = (
        jnp.arange(owners, dtype=jnp.int32)[:, None] < jnp.arange(owners, dtype=jnp.int32)[None, :]
    )
    starts = jnp.sum(jnp.where(before, counts[:, None], 0), axis=0)
    slots = jnp.arange(cap, dtype=jnp.int32)
    places = jnp.where(slots[None, :] < counts[:, None], starts[:, None] + slots[None, :], -1)
    packed_ids = jnp.arange(live_rows, dtype=jnp.int32)
    sides = jnp.arange(2, dtype=jnp.int32)
    side_places = jnp.stack(
        [
            jnp.where(sides[None, :, None] == side, places[:, None, :], -1).reshape(-1)
            for side in range(2)
        ]
    )
    live_targets = jnp.sum(
        jnp.where(packed_ids[:, None] == places.reshape(1, padded), targets[None, :], 0), axis=1
    )

    def both_halves(mine, other, weights):
        half = weights.shape[0] // cores
        part = half // 2
        result = 0.0
        for values, first in ((mine, core * half), (other, (1 - core) * half)):
            for side in range(2):
                result = result + jnp.dot(
                    values[side],
                    lax.dynamic_slice_in_dim(weights, first + side * part, part, axis=0),
                    preferred_element_type=F32,
                )
        return result

    student_rows = spread(group_rows[:, quarter:], "y", lax.axis_size("y"))
    student_rows = student_rows.reshape(2 * padded, -1)
    mine, one = pack_with_places(side_places, student_rows, live_rows)
    partial_logits = both_halves(mine, lax.ppermute(mine, "core", swap), student_head)
    logits_chunk = jnp.sum(
        lax.all_to_all(
            partial_logits.reshape(members, chunk, vocab), "member", 0, 0, tiled=True
        ),
        axis=0,
    )
    student_logits = spread(logits_chunk, "member", members).reshape(live_rows, vocab)
    top, _, total = softmax_stats(logits_chunk)
    vocab_ids = owner * vocab + jnp.arange(vocab, dtype=jnp.int32)
    hit = vocab_ids[None, :] == live_targets[:, None]
    hit_chunk = vocab_ids[None, :] == lax.dynamic_slice_in_dim(
        live_targets, member * chunk, chunk
    )[:, None]
    target_part = jnp.sum(jnp.where(hit_chunk, logits_chunk, 0.0), axis=1)
    student_stats = jnp.concatenate([top, total, target_part, jnp.zeros_like(top)])

    teacher_rows, student_stats = lax.optimization_barrier((teacher_rows, student_stats))
    mine = pack_rows(one, teacher_rows, 2)
    teacher_logits = both_halves(mine, lax.ppermute(mine, "core", swap), teacher_head[0])
    top, shifted, total = softmax_stats(teacher_logits)
    cross = jnp.sum(shifted * student_logits, axis=1)
    shifted = shifted.astype(BF16)
    arrived = [shifted] + [
        lax.ppermute(shifted, "member", [(i, (i + step) % members) for i in range(members)])
        for step in range(1, members)
    ]
    every = spread(jnp.concatenate([top, total, cross, student_stats])[None], OWNERS, owners)
    every = every.reshape(owners, -1)
    student_every = every[:, 3 * live_rows :]
    student_tops = student_every[:, :chunk]
    highest = jnp.max(student_tops, axis=0)
    totals = jnp.sum(
        student_every[:, chunk : 2 * chunk] * jnp.exp(student_tops - highest[None, :]), axis=0
    )
    log_chunk = highest + jnp.log(totals)
    student_loss = jnp.sum(log_chunk) - BLEND * jnp.sum(
        student_every[:, 2 * chunk : 3 * chunk]
    )
    tops = every[:, :live_rows]
    highest = jnp.max(tops, axis=0)
    scales = jnp.exp(tops - highest[None, :])
    totals = jnp.sum(every[:, live_rows : 2 * live_rows] * scales, axis=0)
    crosses = jnp.sum(every[:, 2 * live_rows : 3 * live_rows] * scales, axis=0)
    factor = jnp.exp(top - highest) / totals
    loss = student_loss - (1.0 - BLEND) / members * jnp.sum(crosses / totals)
    factors = spread(
        jnp.concatenate([factor, log_chunk, jnp.full((128 - chunk,), loss)]).reshape(-1, 128), "member", members
    )
    mean_loss = jnp.sum(factors[:, -1, chunk]) / jnp.sum(counts).astype(F32)
    log_total = factors[:, -1, :chunk].reshape(live_rows)
    factors = factors[:, :-1].reshape(members, live_rows)
    ranks = jnp.arange(members, dtype=jnp.int32)[:, None]
    probs = 0.0
    for step in range(members):
        source = (member - step) % members
        scale = jnp.sum(jnp.where(ranks == source, factors, 0.0), axis=0)
        probs = probs + arrived[step].astype(F32) * scale[:, None]
    student_slope = jnp.exp(student_logits - log_total[:, None]) - BLEND * hit.astype(F32)
    slope = (LOSS_SCALE * (student_slope - (1.0 - BLEND) / members * probs)).astype(BF16)

    half = width // 2

    def term(which_core):
        chosen = jnp.take(places.reshape(chips, cores, cap), which_core, axis=1)
        result = 0.0
        for side in range(2):
            at = jnp.where(sides[None, :, None] == side, chosen[:, None, :], -1).reshape(-1, 1)
            unpack = (at == packed_ids[None, :]).astype(BF16)
            rows = jnp.dot(unpack, slope, preferred_element_type=F32).astype(BF16)
            result = result + lax.dot_general(
                rows,
                student_head[side * half : (side + 1) * half],
                (((1,), (1,)), ((), ())),
                preferred_element_type=F32,
            )
        return result

    arrived = lax.ppermute(term(1 - core), "core", swap)
    grads = (term(core) + arrived).astype(BF16).reshape(chips, 2 * cap, half)
    owned = jnp.sum(lax.all_to_all(grads, CHIPS, 0, 0, tiled=True).astype(F32), axis=0)
    slot_grad = jnp.concatenate([owned[:cap], owned[cap:]], axis=1)
    live_here = slots < lax.dynamic_index_in_dim(counts, owner, keepdims=False)
    placed = (
        (jnp.arange(window, dtype=jnp.int32)[:, None] == slot_ids[None, :]) & live_here[None, :]
    ).astype(F32)
    hidden_grad = jnp.sum(placed[:, :, None] * slot_grad[None, :, :], axis=1).astype(BF16)
    return (mean_loss, hidden_grad)


def solution(mesh):
    fine = Mesh(mesh.devices.reshape(4, 8, 8, 2), ("member", "y", "z", "core"))
    placed = (
        P("member", OWNERS, None),
        P("member", None),
        P("member", None, OWNERS),
        P(OWNERS, "member"),
        P("member", OWNERS),
        P(OWNERS, None),
        P(),
        P(),
    )
    return jax.shard_map(
        on_device,
        mesh=fine,
        in_specs=placed,
        out_specs=(P(), P(OWNERS, "member")),
        check_vma=False,
    )
```

```python
import jax
import jax.numpy as jnp
from jax import lax
from jax.experimental import pallas as pl
from jax.experimental.pallas import tpu as pltpu
from jax.sharding import Mesh
from jax.sharding import PartitionSpec as P

LOSS_SCALE = 16.0
BLEND = 0.5
EPS = 1e-05
CHIPS = ("y", "z")
OWNERS = ("y", "z", "core")
BF16 = jnp.bfloat16
F32 = jnp.float32


def spread(block, axes, size):
    return lax.all_to_all(
        jnp.broadcast_to(block[None], (size,) + block.shape), axes, 0, 0, tiled=True
    )


def own_rows_kernel(copies, ids_ref, teacher_ref, gain_ref, student_ref, sent_ref):
    cap = ids_ref.shape[1]
    window, depth = teacher_ref.shape[1:]
    width = student_ref.shape[1]
    rows = 4 * cap
    row = lax.broadcasted_iota(jnp.int32, (rows, window), 0) % cap
    column = lax.broadcasted_iota(jnp.int32, (rows, window), 1)
    wanted = jnp.zeros((rows, window), jnp.int32)
    for slot in range(cap):
        wanted = jnp.where(row == slot, ids_ref[0, slot], wanted)
    select = (column == wanted).astype(BF16)
    picked = jnp.dot(select, teacher_ref[0], preferred_element_type=F32)
    inverse_rms = lax.rsqrt(jnp.mean(picked * picked, axis=1, keepdims=True) + EPS)
    normed = picked * inverse_rms * gain_ref[...]
    student = jnp.dot(select, student_ref[...], preferred_element_type=F32)

    def quarters(values):
        part = values.shape[1] // 4
        group = lax.broadcasted_iota(jnp.int32, (rows, part), 0) // cap
        result = values[:, :part]
        for index in range(1, 4):
            result = jnp.where(group == index, values[:, index * part : (index + 1) * part], result)
        return result.astype(BF16)

    teacher_part, student_part = quarters(normed), quarters(student)
    for copy in range(copies):
        sent_ref[copy * rows : (copy + 1) * rows, : depth // 4] = teacher_part
        sent_ref[copy * rows : (copy + 1) * rows, depth // 4 :] = student_part


def own_rows(copies, slot_ids, teacher_hidden, teacher_gain, student_hidden):
    cap = slot_ids.shape[1]
    features = teacher_hidden.shape[2] // 4 + student_hidden.shape[1] // 4
    return pl.pallas_call(
        lambda *refs: own_rows_kernel(copies, *refs),
        out_shape=jax.ShapeDtypeStruct((copies * 4 * cap, features), BF16),
        in_specs=[pl.BlockSpec(memory_space=pltpu.SMEM)]
        + [pl.BlockSpec(memory_space=pltpu.VMEM)] * 3,
        out_specs=pl.BlockSpec(memory_space=pltpu.VMEM),
        name="own_rows",
    )(slot_ids, teacher_hidden, teacher_gain, student_hidden)


def one_hot_kernel(places_ref, rows_ref, packed_ref, one_ref):
    live = packed_ref.shape[1]
    ids = lax.broadcasted_iota(jnp.int32, (live, places_ref.shape[1]), 0)
    for side in range(2):
        one_ref[side] = (ids == places_ref[side : side + 1, :]).astype(BF16)
        packed_ref[side] = jnp.dot(
            one_ref[side], rows_ref[...], preferred_element_type=F32
        ).astype(BF16)


def pack_with_places(places, rows, live):
    total, features = rows.shape
    return pl.pallas_call(
        one_hot_kernel,
        out_shape=(
            jax.ShapeDtypeStruct((2, live, features), BF16),
            jax.ShapeDtypeStruct((2, live, total), BF16),
        ),
        name="pack_student",
    )(places, rows)


def pack_kernel(one_ref, rows_ref, packed_ref):
    for side in range(2):
        packed_ref[side] = jnp.dot(
            one_ref[side], rows_ref[...], preferred_element_type=F32
        ).astype(BF16)


def pack_rows(one, rows, parts):
    total, features = rows.shape
    live = one.shape[1]
    part = features // parts
    return pl.pallas_call(
        pack_kernel,
        grid=(parts,),
        out_shape=jax.ShapeDtypeStruct((2, live, features), BF16),
        in_specs=[
            pl.BlockSpec((2, live, total), lambda i: (0, 0, 0)),
            pl.BlockSpec((total, part), lambda i: (0, i)),
        ],
        out_specs=pl.BlockSpec((2, live, part), lambda i: (0, 0, i)),
        name="pack_teacher",
    )(one, rows)


def combine_kernel(every_ref, top_ref, sent_ref):
    live = top_ref.shape[1]
    chunk = (every_ref.shape[2] - 2 * live) // 2
    copies = sent_ref.shape[0]

    def totals(first, count):
        tops = every_ref[:, :, first : first + count]
        highest = jnp.max(tops, axis=0)
        sums = every_ref[:, :, first + count : first + 2 * count]
        return highest, jnp.sum(sums * jnp.exp(tops - highest[None]), axis=0)

    highest, total = totals(0, live)
    factor = jnp.exp(top_ref[...] - highest) / total
    highest, total = totals(2 * live, chunk)
    log_total = highest + jnp.log(total)
    for copy in range(copies):
        sent_ref[copy, :, :live] = factor
        sent_ref[copy, :, live:] = jnp.concatenate([log_total, log_total], axis=1)


def combine(every, top, copies):
    live = top.shape[0]
    return pl.pallas_call(
        combine_kernel,
        out_shape=jax.ShapeDtypeStruct((copies, 1, live + 128), F32),
        name="combine",
    )(every, top[None])


def three_parts(values):
    high = lax.reduce_precision(values, 8, 7)
    rest = values - high
    middle = lax.reduce_precision(rest, 8, 7)
    return [part.astype(BF16) for part in (high, middle, rest - middle)]


def softmax_stats(logits):
    top = jnp.max(logits, axis=1)
    shifted = jnp.exp(logits - top[:, None])
    return top, shifted, jnp.sum(shifted, axis=1)


def on_device(
    teacher_hidden,
    teacher_gain,
    teacher_head,
    student_hidden,
    student_head,
    positions,
    counts,
    targets,
):
    members = lax.axis_size("member")
    ring = lax.axis_size("z")
    chips = lax.axis_size("y") * ring
    cores = lax.axis_size("core")
    owners = chips * cores
    member = lax.axis_index("member")
    core = lax.axis_index("core")
    owner = lax.axis_index(OWNERS)
    slot_ids = positions[0]
    cap = slot_ids.shape[0]
    window, width = student_hidden.shape
    vocab = student_head.shape[1]
    padded = owners * cap
    live_rows = padded // 2
    chunk = live_rows // members
    swap = [(0, 1), (1, 0)]

    sent = own_rows(ring, positions, teacher_hidden, teacher_gain, student_hidden)
    depth = teacher_hidden.shape[2]
    quarter = depth // (2 * cores)
    sent = sent.reshape(ring * cores, 2 * cap, -1)
    group_rows = lax.all_to_all(sent, ("z", "core"), 0, 0, tiled=True)
    group_rows = group_rows.reshape(ring * cores * 2 * cap, -1)
    teacher_rows = lax.all_gather(group_rows[:, :quarter], "y", axis=0, tiled=True)

    before = (
        jnp.arange(owners, dtype=jnp.int32)[:, None] < jnp.arange(owners, dtype=jnp.int32)[None, :]
    )
    starts = jnp.sum(jnp.where(before, counts[:, None], 0), axis=0)
    slots = jnp.arange(cap, dtype=jnp.int32)
    places = jnp.where(slots[None, :] < counts[:, None], starts[:, None] + slots[None, :], -1)
    packed_ids = jnp.arange(live_rows, dtype=jnp.int32)
    sides = jnp.arange(2, dtype=jnp.int32)
    side_places = jnp.stack(
        [
            jnp.where(sides[None, :, None] == side, places[:, None, :], -1).reshape(-1)
            for side in range(2)
        ]
    )
    live_targets = jnp.sum(
        jnp.where(packed_ids[:, None] == places.reshape(1, padded), targets[None, :], 0), axis=1
    )

    def both_halves(mine, other, weights):
        half = weights.shape[0] // cores
        part = half // 2
        result = 0.0
        for values, first in ((mine, core * half), (other, (1 - core) * half)):
            for side in range(2):
                result = result + jnp.dot(
                    values[side],
                    lax.dynamic_slice_in_dim(weights, first + side * part, part, axis=0),
                    preferred_element_type=F32,
                )
        return result

    student_rows = spread(group_rows[:, quarter:], "y", lax.axis_size("y"))
    student_rows = student_rows.reshape(2 * padded, -1)
    mine, one = pack_with_places(side_places, student_rows, live_rows)
    partial_logits = both_halves(mine, lax.ppermute(mine, "core", swap), student_head)
    logits_chunk = jnp.sum(
        lax.all_to_all(
            partial_logits.reshape(members, chunk, vocab), "member", 0, 0, tiled=True
        ),
        axis=0,
    )
    student_top, _, student_total = softmax_stats(logits_chunk)
    vocab_ids = owner * vocab + jnp.arange(vocab, dtype=jnp.int32)
    hit = vocab_ids[None, :] == live_targets[:, None]
    teacher_rows, student_top, student_total = lax.optimization_barrier(
        (teacher_rows, student_top, student_total)
    )
    mine = pack_rows(one, teacher_rows, 2)
    teacher_logits = both_halves(mine, lax.ppermute(mine, "core", swap), teacher_head[0])
    top, shifted, total = softmax_stats(teacher_logits)
    every = spread(
        jnp.concatenate([top, total, student_top, student_total])[None], OWNERS, owners
    )
    shared = jnp.concatenate([shifted.astype(BF16)] + three_parts(logits_chunk), axis=0)
    arrived = [shared] + [
        lax.ppermute(shared, "member", [(i, (i + step) % members) for i in range(members)])
        for step in range(1, members)
    ]
    every, *arrived = lax.optimization_barrier((every, *arrived))
    sent = combine(every, top, members)
    factors = lax.all_to_all(sent, "member", 0, 0, tiled=True).reshape(members, -1)
    log_total = factors[:, live_rows : live_rows + chunk].reshape(live_rows)
    factors = factors[:, :live_rows]
    ranks = jnp.arange(members, dtype=jnp.int32)[:, None]
    probs = []
    for step in range(members):
        source = (member - step) % members
        scale = jnp.sum(jnp.where(ranks == source, factors, 0.0), axis=0)
        probs.append(arrived[step][:live_rows].astype(F32) * scale[:, None])
    mean_probs = ((probs[0] + probs[2]) + (probs[1] + probs[3])) / members
    chunks = []
    for index in range(members):
        parts = arrived[0][live_rows:]
        for step in range(1, members):
            parts = jnp.where((member - step) % members == index, arrived[step][live_rows:], parts)
        parts = parts.astype(F32).reshape(3, chunk, vocab)
        chunks.append((parts[0] + parts[1]) + parts[2])
    student_logits = jnp.concatenate(chunks, axis=0)
    mixture = BLEND * hit.astype(F32) + (1.0 - BLEND) * mean_probs
    loss = jnp.where(owner == 0, jnp.sum(log_total), 0.0) - jnp.sum(mixture * student_logits)
    slope = (LOSS_SCALE * (jnp.exp(student_logits - log_total[:, None]) - mixture)).astype(BF16)

    def term(which_core):
        chosen = jnp.take(places.reshape(chips, cores, cap), which_core, axis=1).reshape(-1, 1)
        unpack = (chosen == packed_ids[None, :]).astype(BF16)
        rows = jnp.dot(unpack, slope, preferred_element_type=F32).astype(BF16)
        return lax.dot_general(
            rows, student_head, (((1,), (1,)), ((), ())), preferred_element_type=F32
        )

    arrived = lax.ppermute(term(1 - core), "core", swap)
    other_loss = lax.ppermute(jnp.full((8, 128), loss, F32), "core", swap)
    grads = (term(core) + arrived).reshape(chips, cap, width)
    chip_loss = jnp.broadcast_to(loss + other_loss[0, 0], (chips, cap, 128))
    owned = jnp.sum(
        lax.all_to_all(jnp.concatenate([grads, chip_loss], axis=2), CHIPS, 0, 0, tiled=True),
        axis=0,
    )
    slot_grad = owned[:, :width]
    mean_loss = owned[0, width] / jnp.sum(counts).astype(F32)
    live_here = slots < lax.dynamic_index_in_dim(counts, owner, keepdims=False)
    placed = (
        (jnp.arange(window, dtype=jnp.int32)[:, None] == slot_ids[None, :]) & live_here[None, :]
    ).astype(F32)
    hidden_grad = jnp.sum(placed[:, :, None] * slot_grad[None, :, :], axis=1).astype(BF16)
    return (mean_loss, hidden_grad)


def solution(mesh):
    fine = Mesh(mesh.devices.reshape(4, 8, 8, 2), ("member", "y", "z", "core"))
    placed = (
        P("member", OWNERS, None),
        P("member", None),
        P("member", None, OWNERS),
        P(OWNERS, "member"),
        P("member", OWNERS),
        P(OWNERS, None),
        P(),
        P(),
    )
    return jax.shard_map(
        on_device,
        mesh=fine,
        in_specs=placed,
        out_specs=(P(), P(OWNERS, "member")),
        check_vma=False,
    )
```

```python
import jax
import jax.numpy as jnp
from jax import lax
from jax.experimental import pallas as pl
from jax.experimental.pallas import tpu as pltpu
from jax.sharding import Mesh
from jax.sharding import PartitionSpec as P

LOSS_SCALE = 16.0
BLEND = 0.5
EPS = 1e-05
CHIPS = ("y", "z")
OWNERS = ("y", "z", "core")
BF16 = jnp.bfloat16
F32 = jnp.float32


def spread(block, axes, size):
    return lax.all_to_all(
        jnp.broadcast_to(block[None], (size,) + block.shape), axes, 0, 0, tiled=True
    )


def own_rows_kernel(copies, ids_ref, teacher_ref, gain_ref, student_ref, sent_ref):
    cap = ids_ref.shape[1]
    window, depth = teacher_ref.shape[1:]
    width = student_ref.shape[1]
    rows = 4 * cap
    row = lax.broadcasted_iota(jnp.int32, (rows, window), 0) % cap
    column = lax.broadcasted_iota(jnp.int32, (rows, window), 1)
    wanted = jnp.zeros((rows, window), jnp.int32)
    for slot in range(cap):
        wanted = jnp.where(row == slot, ids_ref[0, slot], wanted)
    select = (column == wanted).astype(BF16)
    picked = jnp.dot(select, teacher_ref[0], preferred_element_type=F32)
    inverse_rms = lax.rsqrt(jnp.mean(picked * picked, axis=1, keepdims=True) + EPS)
    normed = picked * inverse_rms * gain_ref[...]
    student = jnp.dot(select, student_ref[...], preferred_element_type=F32)

    def quarters(values):
        part = values.shape[1] // 4
        group = lax.broadcasted_iota(jnp.int32, (rows, part), 0) // cap
        result = values[:, :part]
        for index in range(1, 4):
            result = jnp.where(group == index, values[:, index * part : (index + 1) * part], result)
        return result.astype(BF16)

    teacher_part, student_part = quarters(normed), quarters(student)
    for copy in range(copies):
        sent_ref[copy * rows : (copy + 1) * rows, : depth // 4] = teacher_part
        sent_ref[copy * rows : (copy + 1) * rows, depth // 4 :] = student_part


def own_rows(copies, slot_ids, teacher_hidden, teacher_gain, student_hidden):
    cap = slot_ids.shape[1]
    features = teacher_hidden.shape[2] // 4 + student_hidden.shape[1] // 4
    return pl.pallas_call(
        lambda *refs: own_rows_kernel(copies, *refs),
        out_shape=jax.ShapeDtypeStruct((copies * 4 * cap, features), BF16),
        in_specs=[pl.BlockSpec(memory_space=pltpu.SMEM)]
        + [pl.BlockSpec(memory_space=pltpu.VMEM)] * 3,
        out_specs=pl.BlockSpec(memory_space=pltpu.VMEM),
        name="own_rows",
    )(slot_ids, teacher_hidden, teacher_gain, student_hidden)


def one_hot_kernel(places_ref, rows_ref, packed_ref, one_ref):
    live = packed_ref.shape[1]
    ids = lax.broadcasted_iota(jnp.int32, (live, places_ref.shape[1]), 0)
    for side in range(2):
        one_ref[side] = (ids == places_ref[side : side + 1, :]).astype(BF16)
        packed_ref[side] = jnp.dot(
            one_ref[side], rows_ref[...], preferred_element_type=F32
        ).astype(BF16)


def pack_with_places(places, rows, live):
    total, features = rows.shape
    return pl.pallas_call(
        one_hot_kernel,
        out_shape=(
            jax.ShapeDtypeStruct((2, live, features), BF16),
            jax.ShapeDtypeStruct((2, live, total), BF16),
        ),
        name="pack_student",
    )(places, rows)


def pack_kernel(one_ref, rows_ref, packed_ref):
    for side in range(2):
        packed_ref[side] = jnp.dot(
            one_ref[side], rows_ref[...], preferred_element_type=F32
        ).astype(BF16)


def pack_rows(one, rows, parts):
    total, features = rows.shape
    live = one.shape[1]
    part = features // parts
    return pl.pallas_call(
        pack_kernel,
        grid=(parts,),
        out_shape=jax.ShapeDtypeStruct((2, live, features), BF16),
        in_specs=[
            pl.BlockSpec((2, live, total), lambda i: (0, 0, 0)),
            pl.BlockSpec((total, part), lambda i: (0, i)),
        ],
        out_specs=pl.BlockSpec((2, live, part), lambda i: (0, 0, i)),
        name="pack_teacher",
    )(one, rows)


def combine_kernel(every_ref, top_ref, sent_ref):
    live = top_ref.shape[1]
    chunk = (every_ref.shape[2] - 2 * live) // 2
    copies = sent_ref.shape[0]

    def totals(first, count):
        tops = every_ref[:, :, first : first + count]
        highest = jnp.max(tops, axis=0)
        sums = every_ref[:, :, first + count : first + 2 * count]
        return highest, jnp.sum(sums * jnp.exp(tops - highest[None]), axis=0)

    highest, total = totals(0, live)
    factor = jnp.exp(top_ref[...] - highest) / total
    highest, total = totals(2 * live, chunk)
    log_total = highest + jnp.log(total)
    for copy in range(copies):
        sent_ref[copy, :, :live] = factor
        sent_ref[copy, :, live:] = jnp.concatenate([log_total, log_total], axis=1)


def combine(every, top, copies):
    live = top.shape[0]
    return pl.pallas_call(
        combine_kernel,
        out_shape=jax.ShapeDtypeStruct((copies, 1, live + 128), F32),
        name="combine",
    )(every, top[None])


def three_parts(values):
    high = lax.reduce_precision(values, 8, 7)
    rest = values - high
    middle = lax.reduce_precision(rest, 8, 7)
    return [part.astype(BF16) for part in (high, middle, rest - middle)]


def softmax_stats(logits):
    top = jnp.max(logits, axis=1)
    shifted = jnp.exp(logits - top[:, None])
    return top, shifted, jnp.sum(shifted, axis=1)


def on_device(
    teacher_hidden,
    teacher_gain,
    teacher_head,
    student_hidden,
    student_head,
    positions,
    counts,
    targets,
):
    members = lax.axis_size("member")
    ring = lax.axis_size("z")
    chips = lax.axis_size("y") * ring
    cores = lax.axis_size("core")
    owners = chips * cores
    member = lax.axis_index("member")
    core = lax.axis_index("core")
    owner = lax.axis_index(OWNERS)
    slot_ids = positions[0]
    cap = slot_ids.shape[0]
    window, width = student_hidden.shape
    vocab = student_head.shape[1]
    padded = owners * cap
    live_rows = padded // 2
    chunk = live_rows // members
    swap = [(0, 1), (1, 0)]

    sent = own_rows(ring, positions, teacher_hidden, teacher_gain, student_hidden)
    depth = teacher_hidden.shape[2]
    quarter = depth // (2 * cores)
    sent = sent.reshape(ring * cores, 2 * cap, -1)
    group_rows = lax.all_to_all(sent, ("z", "core"), 0, 0, tiled=True)
    group_rows = group_rows.reshape(ring * cores * 2 * cap, -1)
    teacher_rows = lax.all_gather(group_rows[:, :quarter], "y", axis=0, tiled=True)

    before = (
        jnp.arange(owners, dtype=jnp.int32)[:, None] < jnp.arange(owners, dtype=jnp.int32)[None, :]
    )
    starts = jnp.sum(jnp.where(before, counts[:, None], 0), axis=0)
    slots = jnp.arange(cap, dtype=jnp.int32)
    places = jnp.where(slots[None, :] < counts[:, None], starts[:, None] + slots[None, :], -1)
    packed_ids = jnp.arange(live_rows, dtype=jnp.int32)
    sides = jnp.arange(2, dtype=jnp.int32)
    side_places = jnp.stack(
        [
            jnp.where(sides[None, :, None] == side, places[:, None, :], -1).reshape(-1)
            for side in range(2)
        ]
    )
    live_targets = jnp.sum(
        jnp.where(packed_ids[:, None] == places.reshape(1, padded), targets[None, :], 0), axis=1
    )

    def both_halves(mine, other, weights):
        half = weights.shape[0] // cores
        part = half // 2
        result = 0.0
        for values, first in ((mine, core * half), (other, (1 - core) * half)):
            for side in range(2):
                result = result + jnp.dot(
                    values[side],
                    lax.dynamic_slice_in_dim(weights, first + side * part, part, axis=0),
                    preferred_element_type=F32,
                )
        return result

    student_rows = spread(group_rows[:, quarter:], "y", lax.axis_size("y"))
    student_rows = student_rows.reshape(2 * padded, -1)
    mine, one = pack_with_places(side_places, student_rows, live_rows)
    partial_logits = both_halves(mine, lax.ppermute(mine, "core", swap), student_head)
    logits_chunk = jnp.sum(
        lax.all_to_all(
            partial_logits.reshape(members, chunk, vocab), "member", 0, 0, tiled=True
        ),
        axis=0,
    )
    student_top, _, student_total = softmax_stats(logits_chunk)
    vocab_ids = owner * vocab + jnp.arange(vocab, dtype=jnp.int32)
    hit = vocab_ids[None, :] == live_targets[:, None]
    teacher_rows, student_top, student_total = lax.optimization_barrier(
        (teacher_rows, student_top, student_total)
    )
    mine = pack_rows(one, teacher_rows, 2)
    teacher_logits = both_halves(mine, lax.ppermute(mine, "core", swap), teacher_head[0])
    top, shifted, total = softmax_stats(teacher_logits)
    every = spread(
        jnp.concatenate([top, total, student_top, student_total])[None], OWNERS, owners
    )
    shared = jnp.concatenate([shifted.astype(BF16)] + three_parts(logits_chunk), axis=0)
    arrived = [shared] + [
        lax.ppermute(shared, "member", [(i, (i + step) % members) for i in range(members)])
        for step in range(1, members)
    ]
    sent = combine(every, top, members)
    factors = lax.all_to_all(sent, "member", 0, 0, tiled=True)
    factors, *arrived = lax.optimization_barrier((factors, *arrived))
    factors = factors.reshape(members, -1)
    log_total = factors[:, live_rows : live_rows + chunk].reshape(live_rows)
    factors = factors[:, :live_rows]
    ranks = jnp.arange(members, dtype=jnp.int32)[:, None]
    probs = []
    for step in range(members):
        source = (member - step) % members
        scale = jnp.sum(jnp.where(ranks == source, factors, 0.0), axis=0)
        probs.append(arrived[step][:live_rows].astype(F32) * scale[:, None])
    mean_probs = ((probs[0] + probs[2]) + (probs[1] + probs[3])) / members
    chunks = []
    for index in range(members):
        parts = arrived[0][live_rows:]
        for step in range(1, members):
            parts = jnp.where((member - step) % members == index, arrived[step][live_rows:], parts)
        parts = parts.astype(F32).reshape(3, chunk, vocab)
        chunks.append((parts[0] + parts[1]) + parts[2])
    student_logits = jnp.concatenate(chunks, axis=0)
    mixture = BLEND * hit.astype(F32) + (1.0 - BLEND) * mean_probs
    loss = jnp.where(owner == 0, jnp.sum(log_total), 0.0) - jnp.sum(mixture * student_logits)
    slope = (LOSS_SCALE * (jnp.exp(student_logits - log_total[:, None]) - mixture)).astype(BF16)

    def term(which_core):
        chosen = jnp.take(places.reshape(chips, cores, cap), which_core, axis=1)
        parts = []
        for slot in range(cap):
            unpack = (chosen[:, slot : slot + 1] == packed_ids[None, :]).astype(BF16)
            rows = jnp.dot(unpack, slope, preferred_element_type=F32).astype(BF16)
            parts.append(
                lax.dot_general(
                    rows, student_head, (((1,), (1,)), ((), ())), preferred_element_type=F32
                )
            )
        return jnp.concatenate(parts + [jnp.full((chips, 128), loss, F32)], axis=1)

    grads = term(core) + lax.ppermute(term(1 - core), "core", swap)
    owned = jnp.sum(lax.all_to_all(grads[:, None, :], CHIPS, 0, 0, tiled=True), axis=0)
    slot_grad = owned[0, : cap * width].reshape(cap, width)
    mean_loss = owned[0, cap * width] / jnp.sum(counts).astype(F32)
    live_here = slots < lax.dynamic_index_in_dim(counts, owner, keepdims=False)
    placed = (
        (jnp.arange(window, dtype=jnp.int32)[:, None] == slot_ids[None, :]) & live_here[None, :]
    ).astype(F32)
    hidden_grad = jnp.sum(placed[:, :, None] * slot_grad[None, :, :], axis=1).astype(BF16)
    return (mean_loss, hidden_grad)


def solution(mesh):
    fine = Mesh(mesh.devices.reshape(4, 8, 8, 2), ("member", "y", "z", "core"))
    placed = (
        P("member", OWNERS, None),
        P("member", None),
        P("member", None, OWNERS),
        P(OWNERS, "member"),
        P("member", OWNERS),
        P(OWNERS, None),
        P(),
        P(),
    )
    return jax.shard_map(
        on_device,
        mesh=fine,
        in_specs=placed,
        out_specs=(P(), P(OWNERS, "member")),
        check_vma=False,
    )
```

```python
import jax
import jax.numpy as jnp
from jax import lax
from jax.experimental import pallas as pl
from jax.experimental.pallas import tpu as pltpu
from jax.sharding import Mesh
from jax.sharding import PartitionSpec as P

LOSS_SCALE = 16.0
BLEND = 0.5
EPS = 1e-05
CHIPS = ("y", "z")
OWNERS = ("y", "z", "core")
BF16 = jnp.bfloat16
F32 = jnp.float32


def spread(block, axes, size):
    return lax.all_to_all(
        jnp.broadcast_to(block[None], (size,) + block.shape), axes, 0, 0, tiled=True
    )


def own_rows_kernel(copies, ids_ref, teacher_ref, gain_ref, student_ref, sent_ref):
    cap = ids_ref.shape[1]
    window, depth = teacher_ref.shape[1:]
    width = student_ref.shape[1]
    rows = 4 * cap
    row = lax.broadcasted_iota(jnp.int32, (rows, window), 0) % cap
    column = lax.broadcasted_iota(jnp.int32, (rows, window), 1)
    wanted = jnp.zeros((rows, window), jnp.int32)
    for slot in range(cap):
        wanted = jnp.where(row == slot, ids_ref[0, slot], wanted)
    select = (column == wanted).astype(BF16)
    picked = jnp.dot(select, teacher_ref[0], preferred_element_type=F32)
    inverse_rms = lax.rsqrt(jnp.mean(picked * picked, axis=1, keepdims=True) + EPS)
    normed = picked * inverse_rms * gain_ref[...]
    student = jnp.dot(select, student_ref[...], preferred_element_type=F32)

    def quarters(values):
        part = values.shape[1] // 4
        group = lax.broadcasted_iota(jnp.int32, (rows, part), 0) // cap
        result = values[:, :part]
        for index in range(1, 4):
            result = jnp.where(group == index, values[:, index * part : (index + 1) * part], result)
        return result.astype(BF16)

    teacher_part, student_part = quarters(normed), quarters(student)
    for copy in range(copies):
        sent_ref[copy * rows : (copy + 1) * rows, : depth // 4] = teacher_part
        sent_ref[copy * rows : (copy + 1) * rows, depth // 4 :] = student_part


def own_rows(copies, slot_ids, teacher_hidden, teacher_gain, student_hidden):
    cap = slot_ids.shape[1]
    features = teacher_hidden.shape[2] // 4 + student_hidden.shape[1] // 4
    return pl.pallas_call(
        lambda *refs: own_rows_kernel(copies, *refs),
        out_shape=jax.ShapeDtypeStruct((copies * 4 * cap, features), BF16),
        in_specs=[pl.BlockSpec(memory_space=pltpu.SMEM)]
        + [pl.BlockSpec(memory_space=pltpu.VMEM)] * 3,
        out_specs=pl.BlockSpec(memory_space=pltpu.VMEM),
        name="own_rows",
    )(slot_ids, teacher_hidden, teacher_gain, student_hidden)


def one_hot_kernel(places_ref, ring_places_ref, rows_ref, packed_ref, one_ref):
    live = packed_ref.shape[1]
    ids = lax.broadcasted_iota(jnp.int32, (live, places_ref.shape[1]), 0)
    for side in range(2):
        one = (ids == places_ref[side : side + 1, :]).astype(BF16)
        packed_ref[side] = jnp.dot(one, rows_ref[...], preferred_element_type=F32).astype(BF16)
        one_ref[side] = (ids == ring_places_ref[side : side + 1, :]).astype(BF16)


def pack_with_places(places, ring_places, rows, live):
    total, features = rows.shape
    return pl.pallas_call(
        one_hot_kernel,
        out_shape=(
            jax.ShapeDtypeStruct((2, live, features), BF16),
            jax.ShapeDtypeStruct((2, live, total), BF16),
        ),
        name="pack_student",
    )(places, ring_places, rows)


def pack_kernel(one_ref, *refs):
    blocks, packed_ref = refs[:-1], refs[-1]
    rows = jnp.concatenate([block[...] for block in blocks], axis=0)
    for side in range(2):
        packed_ref[side] = jnp.dot(one_ref[side], rows, preferred_element_type=F32).astype(BF16)


def pack_rows(one, blocks, parts):
    total = one.shape[2]
    features = blocks[0].shape[1]
    live = one.shape[1]
    part = features // parts
    return pl.pallas_call(
        pack_kernel,
        grid=(parts,),
        out_shape=jax.ShapeDtypeStruct((2, live, features), BF16),
        in_specs=[pl.BlockSpec((2, live, total), lambda i: (0, 0, 0))]
        + [pl.BlockSpec((block.shape[0], part), lambda i: (0, i)) for block in blocks],
        out_specs=pl.BlockSpec((2, live, part), lambda i: (0, 0, i)),
        name="pack_teacher",
    )(one, *blocks)


def both_ways(block, axis, size):
    ahead = [(i, (i + 1) % size) for i in range(size)]
    back = [(i, (i - 1) % size) for i in range(size)]
    result, offsets = [block], [0]
    behind = front = block
    for step in range(1, size // 2):
        behind = lax.ppermute(behind, axis, ahead)
        front = lax.ppermute(front, axis, back)
        result += [behind, front]
        offsets += [-step, step]
    half = block.shape[0] // 2
    result += [
        lax.ppermute(behind[:half], axis, ahead),
        lax.ppermute(front[half:], axis, back),
    ]
    return result, offsets + [size // 2]


def combine_kernel(every_ref, top_ref, sent_ref):
    live = top_ref.shape[1]
    chunk = (every_ref.shape[2] - 2 * live) // 2
    copies = sent_ref.shape[0]

    def totals(first, count):
        tops = every_ref[:, :, first : first + count]
        highest = jnp.max(tops, axis=0)
        sums = every_ref[:, :, first + count : first + 2 * count]
        return highest, jnp.sum(sums * jnp.exp(tops - highest[None]), axis=0)

    highest, total = totals(0, live)
    factor = jnp.exp(top_ref[...] - highest) / total
    highest, total = totals(2 * live, chunk)
    log_total = highest + jnp.log(total)
    for copy in range(copies):
        sent_ref[copy, :, :live] = factor
        sent_ref[copy, :, live:] = jnp.concatenate([log_total, log_total], axis=1)


def combine(every, top, copies):
    live = top.shape[0]
    return pl.pallas_call(
        combine_kernel,
        out_shape=jax.ShapeDtypeStruct((copies, 1, live + 128), F32),
        name="combine",
    )(every, top[None])


def three_parts(values):
    high = lax.reduce_precision(values, 8, 7)
    rest = values - high
    middle = lax.reduce_precision(rest, 8, 7)
    return [part.astype(BF16) for part in (high, middle, rest - middle)]


def softmax_stats(logits):
    top = jnp.max(logits, axis=1)
    shifted = jnp.exp(logits - top[:, None])
    return top, shifted, jnp.sum(shifted, axis=1)


def on_device(
    teacher_hidden,
    teacher_gain,
    teacher_head,
    student_hidden,
    student_head,
    positions,
    counts,
    targets,
):
    members = lax.axis_size("member")
    ring = lax.axis_size("z")
    chips = lax.axis_size("y") * ring
    cores = lax.axis_size("core")
    owners = chips * cores
    member = lax.axis_index("member")
    core = lax.axis_index("core")
    owner = lax.axis_index(OWNERS)
    slot_ids = positions[0]
    cap = slot_ids.shape[0]
    window, width = student_hidden.shape
    vocab = student_head.shape[1]
    padded = owners * cap
    live_rows = padded // 2
    chunk = live_rows // members
    swap = [(0, 1), (1, 0)]

    sent = own_rows(ring, positions, teacher_hidden, teacher_gain, student_hidden)
    depth = teacher_hidden.shape[2]
    quarter = depth // (2 * cores)
    sent = sent.reshape(ring * cores, 2 * cap, -1)
    group_rows = lax.all_to_all(sent, ("z", "core"), 0, 0, tiled=True)
    group_rows = group_rows.reshape(ring * cores * 2 * cap, -1)
    lengths = lax.axis_size("y")
    blocks, offsets = both_ways(group_rows[:, :quarter], "y", lengths)

    before = (
        jnp.arange(owners, dtype=jnp.int32)[:, None] < jnp.arange(owners, dtype=jnp.int32)[None, :]
    )
    starts = jnp.sum(jnp.where(before, counts[:, None], 0), axis=0)
    slots = jnp.arange(cap, dtype=jnp.int32)
    places = jnp.where(slots[None, :] < counts[:, None], starts[:, None] + slots[None, :], -1)
    packed_ids = jnp.arange(live_rows, dtype=jnp.int32)
    sides = jnp.arange(2, dtype=jnp.int32)

    def two_sides(held):
        return jnp.stack(
            [
                jnp.where(sides[None, :, None] == side, held[:, None, :], -1).reshape(-1)
                for side in range(2)
            ]
        )

    sources = (lax.axis_index("y") + jnp.array(offsets, jnp.int32)) % lengths
    ring_places = jnp.take(places.reshape(lengths, -1), sources, axis=0).reshape(owners, cap)
    live_targets = jnp.sum(
        jnp.where(packed_ids[:, None] == places.reshape(1, padded), targets[None, :], 0), axis=1
    )

    def both_halves(mine, other, weights):
        half = weights.shape[0] // cores
        part = half // 2
        result = 0.0
        for values, first in ((mine, core * half), (other, (1 - core) * half)):
            for side in range(2):
                result = result + jnp.dot(
                    values[side],
                    lax.dynamic_slice_in_dim(weights, first + side * part, part, axis=0),
                    preferred_element_type=F32,
                )
        return result

    student_rows = spread(group_rows[:, quarter:], "y", lax.axis_size("y"))
    student_rows = student_rows.reshape(2 * padded, -1)
    mine, one = pack_with_places(
        two_sides(places), two_sides(ring_places), student_rows, live_rows
    )
    partial_logits = both_halves(mine, lax.ppermute(mine, "core", swap), student_head)
    logits_chunk = jnp.sum(
        lax.all_to_all(
            partial_logits.reshape(members, chunk, vocab), "member", 0, 0, tiled=True
        ),
        axis=0,
    )
    student_top, _, student_total = softmax_stats(logits_chunk)
    vocab_ids = owner * vocab + jnp.arange(vocab, dtype=jnp.int32)
    hit = vocab_ids[None, :] == live_targets[:, None]
    student_top, student_total, *blocks = lax.optimization_barrier(
        (student_top, student_total, *blocks)
    )
    mine = pack_rows(one, blocks, 2)
    teacher_logits = both_halves(mine, lax.ppermute(mine, "core", swap), teacher_head[0])
    top, shifted, total = softmax_stats(teacher_logits)
    every = spread(
        jnp.concatenate([top, total, student_top, student_total])[None], OWNERS, owners
    )
    shared = jnp.concatenate([shifted.astype(BF16)] + three_parts(logits_chunk), axis=0)
    arrived = [shared] + [
        lax.ppermute(shared, "member", [(i, (i + step) % members) for i in range(members)])
        for step in range(1, members)
    ]
    sent = combine(every, top, members)
    factors = lax.all_to_all(sent, "member", 0, 0, tiled=True)
    factors, *arrived = lax.optimization_barrier((factors, *arrived))
    factors = factors.reshape(members, -1)
    log_total = factors[:, live_rows : live_rows + chunk].reshape(live_rows)
    factors = factors[:, :live_rows]
    ranks = jnp.arange(members, dtype=jnp.int32)[:, None]
    probs = []
    for step in range(members):
        source = (member - step) % members
        scale = jnp.sum(jnp.where(ranks == source, factors, 0.0), axis=0)
        probs.append(arrived[step][:live_rows].astype(F32) * scale[:, None])
    mean_probs = ((probs[0] + probs[2]) + (probs[1] + probs[3])) / members
    chunks = []
    for index in range(members):
        parts = arrived[0][live_rows:]
        for step in range(1, members):
            parts = jnp.where((member - step) % members == index, arrived[step][live_rows:], parts)
        parts = parts.astype(F32).reshape(3, chunk, vocab)
        chunks.append((parts[0] + parts[1]) + parts[2])
    student_logits = jnp.concatenate(chunks, axis=0)
    mixture = BLEND * hit.astype(F32) + (1.0 - BLEND) * mean_probs
    loss = jnp.where(owner == 0, jnp.sum(log_total), 0.0) - jnp.sum(mixture * student_logits)
    slope = (LOSS_SCALE * (jnp.exp(student_logits - log_total[:, None]) - mixture)).astype(BF16)

    def term(which_core):
        chosen = jnp.take(places.reshape(chips, cores, cap), which_core, axis=1)
        parts = []
        for slot in range(cap):
            unpack = (chosen[:, slot : slot + 1] == packed_ids[None, :]).astype(BF16)
            rows = jnp.dot(unpack, slope, preferred_element_type=F32).astype(BF16)
            parts.append(
                lax.dot_general(
                    rows, student_head, (((1,), (1,)), ((), ())), preferred_element_type=F32
                )
            )
        return jnp.concatenate(parts + [jnp.full((chips, 128), loss, F32)], axis=1)

    grads = term(core) + lax.ppermute(term(1 - core), "core", swap)
    owned = jnp.sum(lax.all_to_all(grads[:, None, :], CHIPS, 0, 0, tiled=True), axis=0)
    slot_grad = owned[0, : cap * width].reshape(cap, width)
    mean_loss = owned[0, cap * width] / jnp.sum(counts).astype(F32)
    live_here = slots < lax.dynamic_index_in_dim(counts, owner, keepdims=False)
    placed = (
        (jnp.arange(window, dtype=jnp.int32)[:, None] == slot_ids[None, :]) & live_here[None, :]
    ).astype(F32)
    hidden_grad = jnp.sum(placed[:, :, None] * slot_grad[None, :, :], axis=1).astype(BF16)
    return (mean_loss, hidden_grad)


def solution(mesh):
    fine = Mesh(mesh.devices.reshape(4, 8, 8, 2), ("member", "y", "z", "core"))
    placed = (
        P("member", OWNERS, None),
        P("member", None),
        P("member", None, OWNERS),
        P(OWNERS, "member"),
        P("member", OWNERS),
        P(OWNERS, None),
        P(),
        P(),
    )
    return jax.shard_map(
        on_device,
        mesh=fine,
        in_specs=placed,
        out_specs=(P(), P(OWNERS, "member")),
        check_vma=False,
    )
```

```python
import jax
import jax.numpy as jnp
from jax import lax
from jax.experimental import pallas as pl
from jax.experimental.pallas import tpu as pltpu
from jax.sharding import Mesh
from jax.sharding import PartitionSpec as P

LOSS_SCALE = 16.0
BLEND = 0.5
EPS = 1e-05
CHIPS = ("y", "z")
OWNERS = ("y", "z", "core")
BF16 = jnp.bfloat16
F32 = jnp.float32
F16 = jnp.float16
GRAD_STEP = 2.0**11
LOSS_STEP = 2.0**-7


def spread(block, axes, size):
    return lax.all_to_all(
        jnp.broadcast_to(block[None], (size,) + block.shape), axes, 0, 0, tiled=True
    )


def own_rows_kernel(copies, ids_ref, teacher_ref, gain_ref, student_ref, sent_ref):
    cap = ids_ref.shape[1]
    window, depth = teacher_ref.shape[1:]
    width = student_ref.shape[1]
    rows = 4 * cap
    row = lax.broadcasted_iota(jnp.int32, (rows, window), 0) % cap
    column = lax.broadcasted_iota(jnp.int32, (rows, window), 1)
    wanted = jnp.zeros((rows, window), jnp.int32)
    for slot in range(cap):
        wanted = jnp.where(row == slot, ids_ref[0, slot], wanted)
    select = (column == wanted).astype(BF16)
    picked = jnp.dot(select, teacher_ref[0], preferred_element_type=F32)
    inverse_rms = lax.rsqrt(jnp.mean(picked * picked, axis=1, keepdims=True) + EPS)
    normed = picked * inverse_rms * gain_ref[...]
    student = jnp.dot(select, student_ref[...], preferred_element_type=F32)

    def quarters(values):
        part = values.shape[1] // 4
        group = lax.broadcasted_iota(jnp.int32, (rows, part), 0) // cap
        result = values[:, :part]
        for index in range(1, 4):
            result = jnp.where(group == index, values[:, index * part : (index + 1) * part], result)
        return result.astype(BF16)

    teacher_part, student_part = quarters(normed), quarters(student)
    for copy in range(copies):
        sent_ref[copy * rows : (copy + 1) * rows, : depth // 4] = teacher_part
        sent_ref[copy * rows : (copy + 1) * rows, depth // 4 :] = student_part


def own_rows(copies, slot_ids, teacher_hidden, teacher_gain, student_hidden):
    cap = slot_ids.shape[1]
    features = teacher_hidden.shape[2] // 4 + student_hidden.shape[1] // 4
    return pl.pallas_call(
        lambda *refs: own_rows_kernel(copies, *refs),
        out_shape=jax.ShapeDtypeStruct((copies * 4 * cap, features), BF16),
        in_specs=[pl.BlockSpec(memory_space=pltpu.SMEM)]
        + [pl.BlockSpec(memory_space=pltpu.VMEM)] * 3,
        out_specs=pl.BlockSpec(memory_space=pltpu.VMEM),
        name="own_rows",
    )(slot_ids, teacher_hidden, teacher_gain, student_hidden)


def one_hot_kernel(places_ref, rows_ref, packed_ref, one_ref):
    live = packed_ref.shape[1]
    ids = lax.broadcasted_iota(jnp.int32, (live, places_ref.shape[1]), 0)
    for side in range(2):
        one_ref[side] = (ids == places_ref[side : side + 1, :]).astype(BF16)
        packed_ref[side] = jnp.dot(
            one_ref[side], rows_ref[...], preferred_element_type=F32
        ).astype(BF16)


def pack_with_places(places, rows, live):
    total, features = rows.shape
    return pl.pallas_call(
        one_hot_kernel,
        out_shape=(
            jax.ShapeDtypeStruct((2, live, features), BF16),
            jax.ShapeDtypeStruct((2, live, total), BF16),
        ),
        name="pack_student",
    )(places, rows)


def pack_kernel(one_ref, rows_ref, packed_ref):
    for side in range(2):
        packed_ref[side] = jnp.dot(
            one_ref[side], rows_ref[...], preferred_element_type=F32
        ).astype(BF16)


def pack_rows(one, rows, parts):
    total, features = rows.shape
    live = one.shape[1]
    part = features // parts
    return pl.pallas_call(
        pack_kernel,
        grid=(parts,),
        out_shape=jax.ShapeDtypeStruct((2, live, features), BF16),
        in_specs=[
            pl.BlockSpec((2, live, total), lambda i: (0, 0, 0)),
            pl.BlockSpec((total, part), lambda i: (0, i)),
        ],
        out_specs=pl.BlockSpec((2, live, part), lambda i: (0, 0, i)),
        name="pack_teacher",
    )(one, rows)


def combine_kernel(every_ref, top_ref, sent_ref):
    live = top_ref.shape[1]
    chunk = (every_ref.shape[2] - 2 * live) // 2
    copies = sent_ref.shape[0]

    def totals(first, count):
        tops = every_ref[:, :, first : first + count]
        highest = jnp.max(tops, axis=0)
        sums = every_ref[:, :, first + count : first + 2 * count]
        return highest, jnp.sum(sums * jnp.exp(tops - highest[None]), axis=0)

    highest, total = totals(0, live)
    factor = jnp.exp(top_ref[...] - highest) / total
    highest, total = totals(2 * live, chunk)
    log_total = highest + jnp.log(total)
    for copy in range(copies):
        sent_ref[copy, :, :live] = factor
        sent_ref[copy, :, live:] = jnp.concatenate([log_total, log_total], axis=1)


def combine(every, top, copies):
    live = top.shape[0]
    return pl.pallas_call(
        combine_kernel,
        out_shape=jax.ShapeDtypeStruct((copies, 1, live + 128), F32),
        name="combine",
    )(every, top[None])


def three_parts(values):
    high = lax.reduce_precision(values, 8, 7)
    rest = values - high
    middle = lax.reduce_precision(rest, 8, 7)
    return [part.astype(BF16) for part in (high, middle, rest - middle)]


def softmax_stats(logits):
    top = jnp.max(logits, axis=1)
    shifted = jnp.exp(logits - top[:, None])
    return top, shifted, jnp.sum(shifted, axis=1)


def on_device(
    teacher_hidden,
    teacher_gain,
    teacher_head,
    student_hidden,
    student_head,
    positions,
    counts,
    targets,
):
    members = lax.axis_size("member")
    ring = lax.axis_size("z")
    chips = lax.axis_size("y") * ring
    cores = lax.axis_size("core")
    owners = chips * cores
    member = lax.axis_index("member")
    core = lax.axis_index("core")
    owner = lax.axis_index(OWNERS)
    slot_ids = positions[0]
    cap = slot_ids.shape[0]
    window, width = student_hidden.shape
    vocab = student_head.shape[1]
    padded = owners * cap
    live_rows = padded // 2
    chunk = live_rows // members
    swap = [(0, 1), (1, 0)]

    sent = own_rows(ring, positions, teacher_hidden, teacher_gain, student_hidden)
    depth = teacher_hidden.shape[2]
    quarter = depth // (2 * cores)
    sent = sent.reshape(ring * cores, 2 * cap, -1)
    group_rows = lax.all_to_all(sent, ("z", "core"), 0, 0, tiled=True)
    group_rows = group_rows.reshape(ring * cores * 2 * cap, -1)
    teacher_rows = lax.all_gather(group_rows[:, :quarter], "y", axis=0, tiled=True)

    before = (
        jnp.arange(owners, dtype=jnp.int32)[:, None] < jnp.arange(owners, dtype=jnp.int32)[None, :]
    )
    starts = jnp.sum(jnp.where(before, counts[:, None], 0), axis=0)
    slots = jnp.arange(cap, dtype=jnp.int32)
    places = jnp.where(slots[None, :] < counts[:, None], starts[:, None] + slots[None, :], -1)
    packed_ids = jnp.arange(live_rows, dtype=jnp.int32)
    sides = jnp.arange(2, dtype=jnp.int32)
    side_places = jnp.stack(
        [
            jnp.where(sides[None, :, None] == side, places[:, None, :], -1).reshape(-1)
            for side in range(2)
        ]
    )
    live_targets = jnp.sum(
        jnp.where(packed_ids[:, None] == places.reshape(1, padded), targets[None, :], 0), axis=1
    )

    def both_halves(mine, other, weights):
        half = weights.shape[0] // cores
        part = half // 2
        result = 0.0
        for values, first in ((mine, core * half), (other, (1 - core) * half)):
            for side in range(2):
                result = result + jnp.dot(
                    values[side],
                    lax.dynamic_slice_in_dim(weights, first + side * part, part, axis=0),
                    preferred_element_type=F32,
                )
        return result

    student_rows = spread(group_rows[:, quarter:], "y", lax.axis_size("y"))
    student_rows = student_rows.reshape(2 * padded, -1)
    mine, one = pack_with_places(side_places, student_rows, live_rows)
    partial_logits = both_halves(mine, lax.ppermute(mine, "core", swap), student_head)
    logits_chunk = jnp.sum(
        lax.all_to_all(
            partial_logits.reshape(members, chunk, vocab), "member", 0, 0, tiled=True
        ),
        axis=0,
    )
    student_top, _, student_total = softmax_stats(logits_chunk)
    vocab_ids = owner * vocab + jnp.arange(vocab, dtype=jnp.int32)
    hit = vocab_ids[None, :] == live_targets[:, None]
    teacher_rows, student_top, student_total = lax.optimization_barrier(
        (teacher_rows, student_top, student_total)
    )
    mine = pack_rows(one, teacher_rows, 2)
    teacher_logits = both_halves(mine, lax.ppermute(mine, "core", swap), teacher_head[0])
    top, shifted, total = softmax_stats(teacher_logits)
    every = spread(
        jnp.concatenate([top, total, student_top, student_total])[None], OWNERS, owners
    )
    shared = jnp.concatenate([shifted.astype(BF16)] + three_parts(logits_chunk), axis=0)
    arrived = [shared] + [
        lax.ppermute(shared, "member", [(i, (i + step) % members) for i in range(members)])
        for step in range(1, members)
    ]
    sent = combine(every, top, members)
    factors = lax.all_to_all(sent, "member", 0, 0, tiled=True)
    factors, *arrived = lax.optimization_barrier((factors, *arrived))
    factors = factors.reshape(members, -1)
    log_total = factors[:, live_rows : live_rows + chunk].reshape(live_rows)
    factors = factors[:, :live_rows]
    ranks = jnp.arange(members, dtype=jnp.int32)[:, None]
    probs = []
    for step in range(members):
        source = (member - step) % members
        scale = jnp.sum(jnp.where(ranks == source, factors, 0.0), axis=0)
        probs.append(arrived[step][:live_rows].astype(F32) * scale[:, None])
    mean_probs = ((probs[0] + probs[2]) + (probs[1] + probs[3])) / members
    chunks = []
    for index in range(members):
        parts = arrived[0][live_rows:]
        for step in range(1, members):
            parts = jnp.where((member - step) % members == index, arrived[step][live_rows:], parts)
        parts = parts.astype(F32).reshape(3, chunk, vocab)
        chunks.append((parts[0] + parts[1]) + parts[2])
    student_logits = jnp.concatenate(chunks, axis=0)
    mixture = BLEND * hit.astype(F32) + (1.0 - BLEND) * mean_probs
    loss = jnp.where(owner == 0, jnp.sum(log_total), 0.0) - jnp.sum(mixture * student_logits)
    slope = (LOSS_SCALE * (jnp.exp(student_logits - log_total[:, None]) - mixture)).astype(BF16)

    half = width // 2

    def term(which_core):
        chosen = jnp.take(places.reshape(chips, cores, cap), which_core, axis=1)
        result = 0.0
        for side in range(2):
            at = jnp.where(sides[None, :, None] == side, chosen[:, None, :], -1).reshape(-1, 1)
            unpack = (at == packed_ids[None, :]).astype(BF16)
            rows = jnp.dot(unpack, slope, preferred_element_type=F32).astype(BF16)
            result = result + lax.dot_general(
                rows,
                student_head[side * half : (side + 1) * half],
                (((1,), (1,)), ((), ())),
                preferred_element_type=F32,
            )
        return jnp.concatenate([result, jnp.full((8, half), loss, F32)], axis=0)

    grads = term(core) + lax.ppermute(term(1 - core), "core", swap)
    chip_loss = grads[-1, 0] * LOSS_STEP
    high = lax.reduce_precision(chip_loss, 5, 10)
    middle = lax.reduce_precision(chip_loss - high, 5, 10)
    parts = jnp.stack([high, middle, (chip_loss - high) - middle]).astype(F16)
    grads = (grads[:-8] * GRAD_STEP).astype(F16).reshape(chips, 2 * cap, half)
    parts = jnp.broadcast_to(jnp.pad(parts, (0, 125)), (chips, 2 * cap, 128))
    owned = lax.all_to_all(jnp.concatenate([grads, parts], axis=2), CHIPS, 0, 0, tiled=True)
    owned = jnp.sum(owned.astype(F32), axis=0)
    slot_grad = jnp.concatenate([owned[:cap, :half], owned[cap:, :half]], axis=1) / GRAD_STEP
    mean_loss = jnp.sum(owned[0, half : half + 3]) / LOSS_STEP / jnp.sum(counts).astype(F32)
    live_here = slots < lax.dynamic_index_in_dim(counts, owner, keepdims=False)
    placed = (
        (jnp.arange(window, dtype=jnp.int32)[:, None] == slot_ids[None, :]) & live_here[None, :]
    ).astype(F32)
    hidden_grad = jnp.sum(placed[:, :, None] * slot_grad[None, :, :], axis=1).astype(BF16)
    return (mean_loss, hidden_grad)


def solution(mesh):
    fine = Mesh(mesh.devices.reshape(4, 8, 8, 2), ("member", "y", "z", "core"))
    placed = (
        P("member", OWNERS, None),
        P("member", None),
        P("member", None, OWNERS),
        P(OWNERS, "member"),
        P("member", OWNERS),
        P(OWNERS, None),
        P(),
        P(),
    )
    return jax.shard_map(
        on_device,
        mesh=fine,
        in_specs=placed,
        out_specs=(P(), P(OWNERS, "member")),
        check_vma=False,
    )
```

```python
import jax
import jax.numpy as jnp
from jax import lax
from jax.experimental import pallas as pl
from jax.experimental.pallas import tpu as pltpu
from jax.sharding import Mesh
from jax.sharding import PartitionSpec as P

LOSS_SCALE = 16.0
BLEND = 0.5
EPS = 1e-05
CHIPS = ("y", "z")
OWNERS = ("y", "z", "core")
BF16 = jnp.bfloat16
F32 = jnp.float32
F16 = jnp.float16
GRAD_STEP = 2.0**11
LOSS_STEP = 2.0**-7


def spread(block, axes, size):
    return lax.all_to_all(
        jnp.broadcast_to(block[None], (size,) + block.shape), axes, 0, 0, tiled=True
    )


def own_rows_kernel(copies, ids_ref, teacher_ref, gain_ref, student_ref, sent_ref):
    cap = ids_ref.shape[1]
    window, depth = teacher_ref.shape[1:]
    width = student_ref.shape[1]
    rows = 4 * cap
    row = lax.broadcasted_iota(jnp.int32, (rows, window), 0) % cap
    column = lax.broadcasted_iota(jnp.int32, (rows, window), 1)
    wanted = jnp.zeros((rows, window), jnp.int32)
    for slot in range(cap):
        wanted = jnp.where(row == slot, ids_ref[0, slot], wanted)
    select = (column == wanted).astype(BF16)
    picked = jnp.dot(select, teacher_ref[0], preferred_element_type=F32)
    inverse_rms = lax.rsqrt(jnp.mean(picked * picked, axis=1, keepdims=True) + EPS)
    normed = picked * inverse_rms * gain_ref[...]
    student = jnp.dot(select, student_ref[...], preferred_element_type=F32)

    def quarters(values):
        part = values.shape[1] // 4
        group = lax.broadcasted_iota(jnp.int32, (rows, part), 0) // cap
        result = values[:, :part]
        for index in range(1, 4):
            result = jnp.where(group == index, values[:, index * part : (index + 1) * part], result)
        return result.astype(BF16)

    teacher_part, student_part = quarters(normed), quarters(student)
    for copy in range(copies):
        sent_ref[copy * rows : (copy + 1) * rows, : depth // 4] = teacher_part
        sent_ref[copy * rows : (copy + 1) * rows, depth // 4 :] = student_part


def own_rows(copies, slot_ids, teacher_hidden, teacher_gain, student_hidden):
    cap = slot_ids.shape[1]
    features = teacher_hidden.shape[2] // 4 + student_hidden.shape[1] // 4
    return pl.pallas_call(
        lambda *refs: own_rows_kernel(copies, *refs),
        out_shape=jax.ShapeDtypeStruct((copies * 4 * cap, features), BF16),
        in_specs=[pl.BlockSpec(memory_space=pltpu.SMEM)]
        + [pl.BlockSpec(memory_space=pltpu.VMEM)] * 3,
        out_specs=pl.BlockSpec(memory_space=pltpu.VMEM),
        name="own_rows",
    )(slot_ids, teacher_hidden, teacher_gain, student_hidden)


def one_hot_kernel(places_ref, rows_ref, packed_ref, one_ref):
    live = packed_ref.shape[1]
    ids = lax.broadcasted_iota(jnp.int32, (live, places_ref.shape[1]), 0)
    for side in range(2):
        one_ref[side] = (ids == places_ref[side : side + 1, :]).astype(BF16)
        packed_ref[side] = jnp.dot(
            one_ref[side], rows_ref[...], preferred_element_type=F32
        ).astype(BF16)


def pack_with_places(places, rows, live):
    total, features = rows.shape
    return pl.pallas_call(
        one_hot_kernel,
        out_shape=(
            jax.ShapeDtypeStruct((2, live, features), BF16),
            jax.ShapeDtypeStruct((2, live, total), BF16),
        ),
        in_specs=[pl.BlockSpec(memory_space=pltpu.VMEM)] * 2,
        out_specs=(pl.BlockSpec(memory_space=pltpu.VMEM),) * 2,
        name="pack_student",
    )(places, rows)


def pack_kernel(one_ref, rows_ref, packed_ref):
    for side in range(2):
        packed_ref[side] = jnp.dot(
            one_ref[side], rows_ref[...], preferred_element_type=F32
        ).astype(BF16)


def pack_rows(one, rows, parts):
    total, features = rows.shape
    live = one.shape[1]
    part = features // parts
    return pl.pallas_call(
        pack_kernel,
        grid=(parts,),
        out_shape=jax.ShapeDtypeStruct((2, live, features), BF16),
        in_specs=[
            pl.BlockSpec((2, live, total), lambda i: (0, 0, 0)),
            pl.BlockSpec((total, part), lambda i: (0, i)),
        ],
        out_specs=pl.BlockSpec((2, live, part), lambda i: (0, 0, i)),
        name="pack_teacher",
    )(one, rows)


def combine_kernel(every_ref, top_ref, sent_ref):
    live = top_ref.shape[1]
    chunk = (every_ref.shape[2] - 2 * live) // 2
    copies = sent_ref.shape[0]

    def totals(first, count):
        tops = every_ref[:, :, first : first + count]
        highest = jnp.max(tops, axis=0)
        sums = every_ref[:, :, first + count : first + 2 * count]
        return highest, jnp.sum(sums * jnp.exp(tops - highest[None]), axis=0)

    highest, total = totals(0, live)
    factor = jnp.exp(top_ref[...] - highest) / total
    highest, total = totals(2 * live, chunk)
    log_total = highest + jnp.log(total)
    for copy in range(copies):
        sent_ref[copy, :, :live] = factor
        sent_ref[copy, :, live:] = jnp.concatenate([log_total, log_total], axis=1)


def combine(every, top, copies):
    live = top.shape[0]
    return pl.pallas_call(
        combine_kernel,
        out_shape=jax.ShapeDtypeStruct((copies, 1, live + 128), F32),
        in_specs=[pl.BlockSpec(memory_space=pltpu.VMEM)] * 2,
        out_specs=pl.BlockSpec(memory_space=pltpu.VMEM),
        name="combine",
    )(every, top[None])


def three_parts(values):
    high = lax.reduce_precision(values, 8, 7)
    rest = values - high
    middle = lax.reduce_precision(rest, 8, 7)
    return [part.astype(BF16) for part in (high, middle, rest - middle)]


def softmax_stats(logits):
    top = jnp.max(logits, axis=1)
    shifted = jnp.exp(logits - top[:, None])
    return top, shifted, jnp.sum(shifted, axis=1)


def on_device(
    teacher_hidden,
    teacher_gain,
    teacher_head,
    student_hidden,
    student_head,
    positions,
    counts,
    targets,
):
    members = lax.axis_size("member")
    ring = lax.axis_size("z")
    chips = lax.axis_size("y") * ring
    cores = lax.axis_size("core")
    owners = chips * cores
    member = lax.axis_index("member")
    core = lax.axis_index("core")
    owner = lax.axis_index(OWNERS)
    slot_ids = positions[0]
    cap = slot_ids.shape[0]
    window, width = student_hidden.shape
    vocab = student_head.shape[1]
    padded = owners * cap
    live_rows = padded // 2
    chunk = live_rows // members
    swap = [(0, 1), (1, 0)]

    sent = own_rows(ring, positions, teacher_hidden, teacher_gain, student_hidden)
    depth = teacher_hidden.shape[2]
    quarter = depth // (2 * cores)
    sent = sent.reshape(ring * cores, 2 * cap, -1)
    group_rows = lax.all_to_all(sent, ("z", "core"), 0, 0, tiled=True)
    group_rows = group_rows.reshape(ring * cores * 2 * cap, -1)
    teacher_rows = lax.all_gather(group_rows[:, :quarter], "y", axis=0, tiled=True)

    before = (
        jnp.arange(owners, dtype=jnp.int32)[:, None] < jnp.arange(owners, dtype=jnp.int32)[None, :]
    )
    starts = jnp.sum(jnp.where(before, counts[:, None], 0), axis=0)
    slots = jnp.arange(cap, dtype=jnp.int32)
    places = jnp.where(slots[None, :] < counts[:, None], starts[:, None] + slots[None, :], -1)
    packed_ids = jnp.arange(live_rows, dtype=jnp.int32)
    sides = jnp.arange(2, dtype=jnp.int32)
    side_places = jnp.stack(
        [
            jnp.where(sides[None, :, None] == side, places[:, None, :], -1).reshape(-1)
            for side in range(2)
        ]
    )
    live_targets = jnp.sum(
        jnp.where(packed_ids[:, None] == places.reshape(1, padded), targets[None, :], 0), axis=1
    )

    def both_halves(mine, other, weights):
        half = weights.shape[0] // cores
        part = half // 2
        result = 0.0
        for values, first in ((mine, core * half), (other, (1 - core) * half)):
            for side in range(2):
                result = result + jnp.dot(
                    values[side],
                    lax.dynamic_slice_in_dim(weights, first + side * part, part, axis=0),
                    preferred_element_type=F32,
                )
        return result

    student_rows = spread(group_rows[:, quarter:], "y", lax.axis_size("y"))
    student_rows = student_rows.reshape(2 * padded, -1)
    mine, one = pack_with_places(side_places, student_rows, live_rows)
    partial_logits = both_halves(mine, lax.ppermute(mine, "core", swap), student_head)
    logits_chunk = jnp.sum(
        lax.all_to_all(
            partial_logits.reshape(members, chunk, vocab), "member", 0, 0, tiled=True
        ),
        axis=0,
    )
    student_top, _, student_total = softmax_stats(logits_chunk)
    vocab_ids = owner * vocab + jnp.arange(vocab, dtype=jnp.int32)
    hit = vocab_ids[None, :] == live_targets[:, None]
    teacher_rows, student_top, student_total = lax.optimization_barrier(
        (teacher_rows, student_top, student_total)
    )
    mine = pack_rows(one, teacher_rows, 2)
    teacher_logits = both_halves(mine, lax.ppermute(mine, "core", swap), teacher_head[0])
    top, shifted, total = softmax_stats(teacher_logits)
    every = spread(
        jnp.concatenate([top, total, student_top, student_total])[None], OWNERS, owners
    )
    shared = jnp.concatenate([shifted.astype(BF16)] + three_parts(logits_chunk), axis=0)
    arrived = [shared] + [
        lax.ppermute(shared, "member", [(i, (i + step) % members) for i in range(members)])
        for step in range(1, members)
    ]
    sent = combine(every, top, members)
    factors = lax.all_to_all(sent, "member", 0, 0, tiled=True)
    factors, *arrived = lax.optimization_barrier((factors, *arrived))
    factors = factors.reshape(members, -1)
    log_total = factors[:, live_rows : live_rows + chunk].reshape(live_rows)
    factors = factors[:, :live_rows]
    ranks = jnp.arange(members, dtype=jnp.int32)[:, None]
    probs = []
    for step in range(members):
        source = (member - step) % members
        scale = jnp.sum(jnp.where(ranks == source, factors, 0.0), axis=0)
        probs.append(arrived[step][:live_rows].astype(F32) * scale[:, None])
    mean_probs = ((probs[0] + probs[2]) + (probs[1] + probs[3])) / members
    chunks = []
    for index in range(members):
        parts = arrived[0][live_rows:]
        for step in range(1, members):
            parts = jnp.where((member - step) % members == index, arrived[step][live_rows:], parts)
        parts = parts.astype(F32).reshape(3, chunk, vocab)
        chunks.append((parts[0] + parts[1]) + parts[2])
    student_logits = jnp.concatenate(chunks, axis=0)
    mixture = BLEND * hit.astype(F32) + (1.0 - BLEND) * mean_probs
    loss = jnp.where(owner == 0, jnp.sum(log_total), 0.0) - jnp.sum(mixture * student_logits)
    slope = (LOSS_SCALE * (jnp.exp(student_logits - log_total[:, None]) - mixture)).astype(BF16)

    half = width // 2

    def term(which_core):
        chosen = jnp.take(places.reshape(chips, cores, cap), which_core, axis=1)
        result = 0.0
        for side in range(2):
            at = jnp.where(sides[None, :, None] == side, chosen[:, None, :], -1).reshape(-1, 1)
            unpack = (at == packed_ids[None, :]).astype(BF16)
            rows = jnp.dot(unpack, slope, preferred_element_type=F32).astype(BF16)
            result = result + lax.dot_general(
                rows,
                student_head[side * half : (side + 1) * half],
                (((1,), (1,)), ((), ())),
                preferred_element_type=F32,
            )
        return jnp.concatenate([result, jnp.full((8, half), loss, F32)], axis=0)

    grads = term(core) + lax.ppermute(term(1 - core), "core", swap)
    chip_loss = grads[-8:] * LOSS_STEP
    high = lax.reduce_precision(chip_loss, 5, 10)
    middle = lax.reduce_precision(chip_loss - high, 5, 10)
    low = (chip_loss - high) - middle
    row = lax.broadcasted_iota(jnp.int32, chip_loss.shape, 0)
    parts = jnp.where(row == 0, high, jnp.where(row == 1, middle, low)).astype(F16)
    grads = (grads[:-8] * GRAD_STEP).astype(F16).reshape(chips, 2 * cap, half)
    parts = jnp.broadcast_to(parts[None], (chips, 8, half))
    owned = lax.all_to_all(jnp.concatenate([grads, parts], axis=1), CHIPS, 0, 0, tiled=True)
    owned = jnp.sum(owned.astype(F32), axis=0)
    slot_grad = jnp.concatenate([owned[:cap], owned[cap : 2 * cap]], axis=1) / GRAD_STEP
    mean_loss = jnp.sum(owned[2 * cap : 2 * cap + 3, 0]) / LOSS_STEP
    mean_loss = mean_loss / jnp.sum(counts).astype(F32)
    live_here = slots < lax.dynamic_index_in_dim(counts, owner, keepdims=False)
    placed = (
        (jnp.arange(window, dtype=jnp.int32)[:, None] == slot_ids[None, :]) & live_here[None, :]
    ).astype(F32)
    hidden_grad = jnp.sum(placed[:, :, None] * slot_grad[None, :, :], axis=1).astype(BF16)
    return (mean_loss, hidden_grad)


def solution(mesh):
    fine = Mesh(mesh.devices.reshape(4, 8, 8, 2), ("member", "y", "z", "core"))
    placed = (
        P("member", OWNERS, None),
        P("member", None),
        P("member", None, OWNERS),
        P(OWNERS, "member"),
        P("member", OWNERS),
        P(OWNERS, None),
        P(),
        P(),
    )
    return jax.shard_map(
        on_device,
        mesh=fine,
        in_specs=placed,
        out_specs=(P(), P(OWNERS, "member")),
        check_vma=False,
    )
```

```python
import jax
import jax.numpy as jnp
from jax import lax
from jax.experimental import pallas as pl
from jax.experimental.pallas import tpu as pltpu
from jax.sharding import Mesh
from jax.sharding import PartitionSpec as P

LOSS_SCALE = 16.0
BLEND = 0.5
EPS = 1e-05
CHIPS = ("y", "z")
OWNERS = ("y", "z", "core")
BF16 = jnp.bfloat16
F32 = jnp.float32
F16 = jnp.float16
GRAD_STEP = 2.0**11


def spread(block, axes, size):
    return lax.all_to_all(
        jnp.broadcast_to(block[None], (size,) + block.shape), axes, 0, 0, tiled=True
    )


def own_rows_kernel(copies, ids_ref, teacher_ref, gain_ref, student_ref, sent_ref):
    cap = ids_ref.shape[1]
    window, depth = teacher_ref.shape[1:]
    width = student_ref.shape[1]
    rows = 4 * cap
    row = lax.broadcasted_iota(jnp.int32, (rows, window), 0) % cap
    column = lax.broadcasted_iota(jnp.int32, (rows, window), 1)
    wanted = jnp.zeros((rows, window), jnp.int32)
    for slot in range(cap):
        wanted = jnp.where(row == slot, ids_ref[0, slot], wanted)
    select = (column == wanted).astype(BF16)
    picked = jnp.dot(select, teacher_ref[0], preferred_element_type=F32)
    inverse_rms = lax.rsqrt(jnp.mean(picked * picked, axis=1, keepdims=True) + EPS)
    normed = picked * inverse_rms * gain_ref[...]
    student = jnp.dot(select, student_ref[...], preferred_element_type=F32)

    def quarters(values):
        part = values.shape[1] // 4
        group = lax.broadcasted_iota(jnp.int32, (rows, part), 0) // cap
        result = values[:, :part]
        for index in range(1, 4):
            result = jnp.where(group == index, values[:, index * part : (index + 1) * part], result)
        return result.astype(BF16)

    teacher_part, student_part = quarters(normed), quarters(student)
    for copy in range(copies):
        sent_ref[copy * rows : (copy + 1) * rows, : depth // 4] = teacher_part
        sent_ref[copy * rows : (copy + 1) * rows, depth // 4 :] = student_part


def own_rows(copies, slot_ids, teacher_hidden, teacher_gain, student_hidden):
    cap = slot_ids.shape[1]
    features = teacher_hidden.shape[2] // 4 + student_hidden.shape[1] // 4
    return pl.pallas_call(
        lambda *refs: own_rows_kernel(copies, *refs),
        out_shape=jax.ShapeDtypeStruct((copies * 4 * cap, features), BF16),
        in_specs=[pl.BlockSpec(memory_space=pltpu.SMEM)]
        + [pl.BlockSpec(memory_space=pltpu.VMEM)] * 3,
        out_specs=pl.BlockSpec(memory_space=pltpu.VMEM),
        name="own_rows",
    )(slot_ids, teacher_hidden, teacher_gain, student_hidden)


def one_hot_kernel(places_ref, rows_ref, packed_ref, one_ref):
    live = packed_ref.shape[1]
    ids = lax.broadcasted_iota(jnp.int32, (live, places_ref.shape[1]), 0)
    for side in range(2):
        one_ref[side] = (ids == places_ref[side : side + 1, :]).astype(BF16)
        packed_ref[side] = jnp.dot(
            one_ref[side], rows_ref[...], preferred_element_type=F32
        ).astype(BF16)


def pack_with_places(places, rows, live):
    total, features = rows.shape
    return pl.pallas_call(
        one_hot_kernel,
        out_shape=(
            jax.ShapeDtypeStruct((2, live, features), BF16),
            jax.ShapeDtypeStruct((2, live, total), BF16),
        ),
        name="pack_student",
    )(places, rows)


def pack_kernel(one_ref, rows_ref, packed_ref):
    for side in range(2):
        packed_ref[side] = jnp.dot(
            one_ref[side], rows_ref[...], preferred_element_type=F32
        ).astype(BF16)


def pack_rows(one, rows, parts):
    total, features = rows.shape
    live = one.shape[1]
    part = features // parts
    return pl.pallas_call(
        pack_kernel,
        grid=(parts,),
        out_shape=jax.ShapeDtypeStruct((2, live, features), BF16),
        in_specs=[
            pl.BlockSpec((2, live, total), lambda i: (0, 0, 0)),
            pl.BlockSpec((total, part), lambda i: (0, i)),
        ],
        out_specs=pl.BlockSpec((2, live, part), lambda i: (0, 0, i)),
        cost_estimate=pl.CostEstimate(
            flops=4 * live * total * features, bytes_accessed=8 << 20, transcendentals=0
        ),
        name="pack_teacher",
    )(one, rows)


def combine_kernel(every_ref, top_ref, sent_ref):
    live = top_ref.shape[1]
    chunk = (every_ref.shape[2] - 3 * live) // 4
    copies = sent_ref.shape[0]

    def scaled(first, count, sums):
        tops = every_ref[:, :, first : first + count]
        highest = jnp.max(tops, axis=0)
        scales = jnp.exp(tops - highest[None])
        starts = [first + (1 + index) * count for index in range(sums)]
        return highest, [
            jnp.sum(every_ref[:, :, start : start + count] * scales, axis=0) for start in starts
        ]

    highest, (total, cross) = scaled(0, live, 2)
    factor = jnp.exp(top_ref[...] - highest) / total
    crosses = jnp.sum(cross / total, axis=1, keepdims=True)
    first = 3 * live
    highest, (total,) = scaled(first, chunk, 1)
    log_total = highest + jnp.log(total)
    hits = jnp.sum(every_ref[:, :, first + 2 * chunk : first + 3 * chunk], axis=0)
    loss = (
        jnp.sum(log_total, axis=1, keepdims=True)
        - BLEND * jnp.sum(hits, axis=1, keepdims=True)
        - (1.0 - BLEND) / copies * crosses
    )
    tail = jnp.concatenate([log_total, jnp.broadcast_to(loss, (1, chunk))], axis=1)
    for copy in range(copies):
        sent_ref[copy, :, :live] = factor
        sent_ref[copy, :, live:] = tail


def combine(every, top, copies):
    live = top.shape[0]
    return pl.pallas_call(
        combine_kernel,
        out_shape=jax.ShapeDtypeStruct((copies, 1, live + 128), F32),
        name="combine",
    )(every, top[None])


def softmax_stats(logits):
    top = jnp.max(logits, axis=1)
    shifted = jnp.exp(logits - top[:, None])
    return top, shifted, jnp.sum(shifted, axis=1)


def on_device(
    teacher_hidden,
    teacher_gain,
    teacher_head,
    student_hidden,
    student_head,
    positions,
    counts,
    targets,
):
    members = lax.axis_size("member")
    ring = lax.axis_size("z")
    chips = lax.axis_size("y") * ring
    cores = lax.axis_size("core")
    owners = chips * cores
    member = lax.axis_index("member")
    core = lax.axis_index("core")
    owner = lax.axis_index(OWNERS)
    slot_ids = positions[0]
    cap = slot_ids.shape[0]
    window, width = student_hidden.shape
    vocab = student_head.shape[1]
    padded = owners * cap
    live_rows = padded // 2
    chunk = live_rows // members
    swap = [(0, 1), (1, 0)]

    sent = own_rows(ring, positions, teacher_hidden, teacher_gain, student_hidden)
    depth = teacher_hidden.shape[2]
    quarter = depth // (2 * cores)
    sent = sent.reshape(ring * cores, 2 * cap, -1)
    group_rows = lax.all_to_all(sent, ("z", "core"), 0, 0, tiled=True)
    group_rows = group_rows.reshape(ring * cores * 2 * cap, -1)
    teacher_rows = lax.all_gather(group_rows[:, :quarter], "y", axis=0, tiled=True)

    before = (
        jnp.arange(owners, dtype=jnp.int32)[:, None] < jnp.arange(owners, dtype=jnp.int32)[None, :]
    )
    starts = jnp.sum(jnp.where(before, counts[:, None], 0), axis=0)
    slots = jnp.arange(cap, dtype=jnp.int32)
    places = jnp.where(slots[None, :] < counts[:, None], starts[:, None] + slots[None, :], -1)
    packed_ids = jnp.arange(live_rows, dtype=jnp.int32)
    sides = jnp.arange(2, dtype=jnp.int32)
    side_places = jnp.stack(
        [
            jnp.where(sides[None, :, None] == side, places[:, None, :], -1).reshape(-1)
            for side in range(2)
        ]
    )
    live_targets = jnp.sum(
        jnp.where(packed_ids[:, None] == places.reshape(1, padded), targets[None, :], 0), axis=1
    )

    def both_halves(mine, other, weights):
        half = weights.shape[0] // cores
        part = half // 2
        result = 0.0
        for values, first in ((mine, core * half), (other, (1 - core) * half)):
            for side in range(2):
                result = result + jnp.dot(
                    values[side],
                    lax.dynamic_slice_in_dim(weights, first + side * part, part, axis=0),
                    preferred_element_type=F32,
                )
        return result

    student_rows = spread(group_rows[:, quarter:], "y", lax.axis_size("y"))
    student_rows = student_rows.reshape(2 * padded, -1)
    mine, one = pack_with_places(side_places, student_rows, live_rows)
    partial_logits = both_halves(mine, lax.ppermute(mine, "core", swap), student_head)
    logits_chunk = jnp.sum(
        lax.all_to_all(
            partial_logits.reshape(members, chunk, vocab), "member", 0, 0, tiled=True
        ),
        axis=0,
    )
    student_logits = spread(logits_chunk, "member", members).reshape(live_rows, vocab)
    top, _, total = softmax_stats(logits_chunk)
    vocab_ids = owner * vocab + jnp.arange(vocab, dtype=jnp.int32)
    hit = vocab_ids[None, :] == live_targets[:, None]
    hit_chunk = vocab_ids[None, :] == lax.dynamic_slice_in_dim(
        live_targets, member * chunk, chunk
    )[:, None]
    target_part = jnp.sum(jnp.where(hit_chunk, logits_chunk, 0.0), axis=1)
    student_stats = jnp.concatenate([top, total, target_part, jnp.zeros_like(top)])

    teacher_rows, student_stats = lax.optimization_barrier((teacher_rows, student_stats))
    mine = pack_rows(one, teacher_rows, 2)
    teacher_logits = both_halves(mine, lax.ppermute(mine, "core", swap), teacher_head[0])
    top, shifted, total = softmax_stats(teacher_logits)
    cross = jnp.sum(shifted * student_logits, axis=1)
    shifted = shifted.astype(BF16)
    arrived = [shifted] + [
        lax.ppermute(shifted, "member", [(i, (i + step) % members) for i in range(members)])
        for step in range(1, members)
    ]
    every = spread(jnp.concatenate([top, total, cross, student_stats])[None], OWNERS, owners)
    factors = lax.all_to_all(combine(every, top, members), "member", 0, 0, tiled=True)
    factors = factors.reshape(members, -1)
    mean_loss = jnp.sum(factors[:, live_rows + chunk]) / jnp.sum(counts).astype(F32)
    log_total = factors[:, live_rows : live_rows + chunk].reshape(live_rows)
    factors = factors[:, :live_rows]
    ranks = jnp.arange(members, dtype=jnp.int32)[:, None]
    probs = 0.0
    for step in range(members):
        source = (member - step) % members
        scale = jnp.sum(jnp.where(ranks == source, factors, 0.0), axis=0)
        probs = probs + arrived[step].astype(F32) * scale[:, None]
    student_slope = jnp.exp(student_logits - log_total[:, None]) - BLEND * hit.astype(F32)
    slope = (LOSS_SCALE * (student_slope - (1.0 - BLEND) / members * probs)).astype(BF16)

    half = width // 2

    def term(which_core):
        chosen = jnp.take(places.reshape(chips, cores, cap), which_core, axis=1)
        result = 0.0
        for side in range(2):
            at = jnp.where(sides[None, :, None] == side, chosen[:, None, :], -1).reshape(-1, 1)
            unpack = (at == packed_ids[None, :]).astype(BF16)
            rows = jnp.dot(unpack, slope, preferred_element_type=F32).astype(BF16)
            result = result + lax.dot_general(
                rows,
                student_head[side * half : (side + 1) * half],
                (((1,), (1,)), ((), ())),
                preferred_element_type=F32,
            )
        return result

    arrived = lax.ppermute(term(1 - core), "core", swap)
    grads = ((term(core) + arrived) * GRAD_STEP).astype(F16).reshape(chips, 2 * cap, half)
    owned = jnp.sum(lax.all_to_all(grads, CHIPS, 0, 0, tiled=True).astype(F32), axis=0)
    slot_grad = jnp.concatenate([owned[:cap], owned[cap:]], axis=1) / GRAD_STEP
    live_here = slots < lax.dynamic_index_in_dim(counts, owner, keepdims=False)
    placed = (
        (jnp.arange(window, dtype=jnp.int32)[:, None] == slot_ids[None, :]) & live_here[None, :]
    ).astype(F32)
    hidden_grad = jnp.sum(placed[:, :, None] * slot_grad[None, :, :], axis=1).astype(BF16)
    return (mean_loss, hidden_grad)


def solution(mesh):
    fine = Mesh(mesh.devices.reshape(4, 8, 8, 2), ("member", "y", "z", "core"))
    placed = (
        P("member", OWNERS, None),
        P("member", None),
        P("member", None, OWNERS),
        P(OWNERS, "member"),
        P("member", OWNERS),
        P(OWNERS, None),
        P(),
        P(),
    )
    return jax.shard_map(
        on_device,
        mesh=fine,
        in_specs=placed,
        out_specs=(P(), P(OWNERS, "member")),
        check_vma=False,
    )
```

```python
import jax
import jax.numpy as jnp
from jax import lax
from jax.experimental import pallas as pl
from jax.experimental.pallas import tpu as pltpu
from jax.sharding import Mesh
from jax.sharding import PartitionSpec as P

LOSS_SCALE = 16.0
BLEND = 0.5
EPS = 1e-05
CHIPS = ("y", "z")
OWNERS = ("y", "z", "core")
BF16 = jnp.bfloat16
F32 = jnp.float32
F16 = jnp.float16
GRAD_STEP = 2.0**11


def spread(block, axes, size):
    return lax.all_to_all(
        jnp.broadcast_to(block[None], (size,) + block.shape), axes, 0, 0, tiled=True
    )


def own_rows_kernel(copies, ids_ref, teacher_ref, gain_ref, student_ref, sent_ref):
    cap = ids_ref.shape[1]
    window, depth = teacher_ref.shape[1:]
    width = student_ref.shape[1]
    rows = 4 * cap
    row = lax.broadcasted_iota(jnp.int32, (rows, window), 0) % cap
    column = lax.broadcasted_iota(jnp.int32, (rows, window), 1)
    wanted = jnp.zeros((rows, window), jnp.int32)
    for slot in range(cap):
        wanted = jnp.where(row == slot, ids_ref[0, slot], wanted)
    select = (column == wanted).astype(BF16)
    picked = jnp.dot(select, teacher_ref[0], preferred_element_type=F32)
    inverse_rms = lax.rsqrt(jnp.mean(picked * picked, axis=1, keepdims=True) + EPS)
    normed = picked * inverse_rms * gain_ref[...]
    student = jnp.dot(select, student_ref[...], preferred_element_type=F32)

    def quarters(values):
        part = values.shape[1] // 4
        group = lax.broadcasted_iota(jnp.int32, (rows, part), 0) // cap
        result = values[:, :part]
        for index in range(1, 4):
            result = jnp.where(group == index, values[:, index * part : (index + 1) * part], result)
        return result.astype(BF16)

    teacher_part, student_part = quarters(normed), quarters(student)
    for copy in range(copies):
        sent_ref[copy * rows : (copy + 1) * rows, : depth // 4] = teacher_part
        sent_ref[copy * rows : (copy + 1) * rows, depth // 4 :] = student_part


def own_rows(copies, slot_ids, teacher_hidden, teacher_gain, student_hidden):
    cap = slot_ids.shape[1]
    features = teacher_hidden.shape[2] // 4 + student_hidden.shape[1] // 4
    return pl.pallas_call(
        lambda *refs: own_rows_kernel(copies, *refs),
        out_shape=jax.ShapeDtypeStruct((copies * 4 * cap, features), BF16),
        in_specs=[pl.BlockSpec(memory_space=pltpu.SMEM)]
        + [pl.BlockSpec(memory_space=pltpu.VMEM)] * 3,
        out_specs=pl.BlockSpec(memory_space=pltpu.VMEM),
        name="own_rows",
    )(slot_ids, teacher_hidden, teacher_gain, student_hidden)


def one_hot_kernel(places_ref, rows_ref, packed_ref, one_ref):
    live = packed_ref.shape[1]
    ids = lax.broadcasted_iota(jnp.int32, (live, places_ref.shape[1]), 0)
    for side in range(2):
        one_ref[side] = (ids == places_ref[side : side + 1, :]).astype(BF16)
        packed_ref[side] = jnp.dot(
            one_ref[side], rows_ref[...], preferred_element_type=F32
        ).astype(BF16)


def pack_with_places(places, rows, live):
    total, features = rows.shape
    return pl.pallas_call(
        one_hot_kernel,
        out_shape=(
            jax.ShapeDtypeStruct((2, live, features), BF16),
            jax.ShapeDtypeStruct((2, live, total), BF16),
        ),
        name="pack_student",
    )(places, rows)


def pack_kernel(one_ref, rows_ref, packed_ref):
    for side in range(2):
        packed_ref[side] = jnp.dot(
            one_ref[side], rows_ref[...], preferred_element_type=F32
        ).astype(BF16)


def pack_rows(one, rows, parts):
    total, features = rows.shape
    live = one.shape[1]
    part = features // parts
    return pl.pallas_call(
        pack_kernel,
        grid=(parts,),
        out_shape=jax.ShapeDtypeStruct((2, live, features), BF16),
        in_specs=[
            pl.BlockSpec((2, live, total), lambda i: (0, 0, 0)),
            pl.BlockSpec((total, part), lambda i: (0, i)),
        ],
        out_specs=pl.BlockSpec((2, live, part), lambda i: (0, 0, i)),
        cost_estimate=pl.CostEstimate(
            flops=4 * live * total * features, bytes_accessed=8 << 20, transcendentals=0
        ),
        name="pack_teacher",
    )(one, rows)


def combine_kernel(every_ref, top_ref, sent_ref):
    live = top_ref.shape[1]
    chunk = (every_ref.shape[2] - 3 * live) // 3
    copies = sent_ref.shape[0]

    def scaled(first, count, sums):
        tops = every_ref[:, :, first : first + count]
        highest = jnp.max(tops, axis=0)
        scales = jnp.exp(tops - highest[None])
        starts = [first + (1 + index) * count for index in range(sums)]
        return highest, [
            jnp.sum(every_ref[:, :, start : start + count] * scales, axis=0) for start in starts
        ]

    highest, (total, cross) = scaled(0, live, 2)
    factor = jnp.exp(top_ref[...] - highest) / total
    crosses = jnp.sum(cross / total, axis=1, keepdims=True)
    first = 3 * live
    highest, (total,) = scaled(first, chunk, 1)
    log_total = highest + jnp.log(total)
    hits = jnp.sum(every_ref[:, :, first + 2 * chunk : first + 3 * chunk], axis=0)
    loss = (
        jnp.sum(log_total, axis=1, keepdims=True)
        - BLEND * jnp.sum(hits, axis=1, keepdims=True)
        - (1.0 - BLEND) / copies * crosses
    )
    tail = jnp.concatenate([log_total, jnp.broadcast_to(loss, (1, chunk))], axis=1)
    for copy in range(copies):
        sent_ref[copy, :, :live] = factor
        sent_ref[copy, :, live:] = tail


def combine(every, top, copies):
    live = top.shape[0]
    return pl.pallas_call(
        combine_kernel,
        out_shape=jax.ShapeDtypeStruct((copies, 1, live + 128), F32),
        name="combine",
    )(every, top[None])


def softmax_stats(logits):
    top = jnp.max(logits, axis=1)
    shifted = jnp.exp(logits - top[:, None])
    return top, shifted, jnp.sum(shifted, axis=1)


def on_device(
    teacher_hidden,
    teacher_gain,
    teacher_head,
    student_hidden,
    student_head,
    positions,
    counts,
    targets,
):
    members = lax.axis_size("member")
    ring = lax.axis_size("z")
    chips = lax.axis_size("y") * ring
    cores = lax.axis_size("core")
    owners = chips * cores
    member = lax.axis_index("member")
    core = lax.axis_index("core")
    owner = lax.axis_index(OWNERS)
    slot_ids = positions[0]
    cap = slot_ids.shape[0]
    window, width = student_hidden.shape
    vocab = student_head.shape[1]
    padded = owners * cap
    live_rows = padded // 2
    chunk = live_rows // members
    swap = [(0, 1), (1, 0)]

    sent = own_rows(ring, positions, teacher_hidden, teacher_gain, student_hidden)
    depth = teacher_hidden.shape[2]
    quarter = depth // (2 * cores)
    sent = sent.reshape(ring * cores, 2 * cap, -1)
    group_rows = lax.all_to_all(sent, ("z", "core"), 0, 0, tiled=True)
    group_rows = group_rows.reshape(ring * cores * 2 * cap, -1)
    teacher_rows = lax.all_gather(group_rows[:, :quarter], "y", axis=0, tiled=True)

    before = (
        jnp.arange(owners, dtype=jnp.int32)[:, None] < jnp.arange(owners, dtype=jnp.int32)[None, :]
    )
    starts = jnp.sum(jnp.where(before, counts[:, None], 0), axis=0)
    slots = jnp.arange(cap, dtype=jnp.int32)
    places = jnp.where(slots[None, :] < counts[:, None], starts[:, None] + slots[None, :], -1)
    packed_ids = jnp.arange(live_rows, dtype=jnp.int32)
    sides = jnp.arange(2, dtype=jnp.int32)
    side_places = jnp.stack(
        [
            jnp.where(sides[None, :, None] == side, places[:, None, :], -1).reshape(-1)
            for side in range(2)
        ]
    )
    live_targets = jnp.sum(
        jnp.where(packed_ids[:, None] == places.reshape(1, padded), targets[None, :], 0), axis=1
    )

    def both_halves(mine, other, weights):
        half = weights.shape[0] // cores
        part = half // 2
        result = 0.0
        for values, first in ((mine, core * half), (other, (1 - core) * half)):
            for side in range(2):
                result = result + jnp.dot(
                    values[side],
                    lax.dynamic_slice_in_dim(weights, first + side * part, part, axis=0),
                    preferred_element_type=F32,
                )
        return result

    student_rows = spread(group_rows[:, quarter:], "y", lax.axis_size("y"))
    student_rows = student_rows.reshape(2 * padded, -1)
    mine, one = pack_with_places(side_places, student_rows, live_rows)
    partial_logits = both_halves(mine, lax.ppermute(mine, "core", swap), student_head)
    logits_chunk = jnp.sum(
        lax.all_to_all(
            partial_logits.reshape(members, chunk, vocab), "member", 0, 0, tiled=True
        ),
        axis=0,
    )
    student_logits = spread(logits_chunk, "member", members).reshape(live_rows, vocab)
    top, _, total = softmax_stats(logits_chunk)
    vocab_ids = owner * vocab + jnp.arange(vocab, dtype=jnp.int32)
    hit = vocab_ids[None, :] == live_targets[:, None]
    hit_chunk = vocab_ids[None, :] == lax.dynamic_slice_in_dim(
        live_targets, member * chunk, chunk
    )[:, None]
    target_part = jnp.sum(jnp.where(hit_chunk, logits_chunk, 0.0), axis=1)
    student_stats = jnp.concatenate([top, total, target_part])

    teacher_rows, student_stats = lax.optimization_barrier((teacher_rows, student_stats))
    mine = pack_rows(one, teacher_rows, 4)
    teacher_logits = both_halves(mine, lax.ppermute(mine, "core", swap), teacher_head[0])
    top, shifted, total = softmax_stats(teacher_logits)
    cross = jnp.sum(shifted * student_logits, axis=1)
    shifted = shifted.astype(BF16)
    arrived = [shifted] + [
        lax.ppermute(shifted, "member", [(i, (i + step) % members) for i in range(members)])
        for step in range(1, members)
    ]
    every = spread(jnp.concatenate([top, total, cross, student_stats])[None], OWNERS, owners)
    factors = lax.all_to_all(combine(every, top, members), "member", 0, 0, tiled=True)
    factors = factors.reshape(members, -1)
    mean_loss = jnp.sum(factors[:, live_rows + chunk]) / jnp.sum(counts).astype(F32)
    log_total = factors[:, live_rows : live_rows + chunk].reshape(live_rows)
    factors = factors[:, :live_rows]
    ranks = jnp.arange(members, dtype=jnp.int32)[:, None]
    probs = 0.0
    for step in range(members):
        source = (member - step) % members
        scale = jnp.sum(jnp.where(ranks == source, factors, 0.0), axis=0)
        probs = probs + arrived[step].astype(F32) * scale[:, None]
    student_slope = jnp.exp(student_logits - log_total[:, None]) - BLEND * hit.astype(F32)
    slope = (LOSS_SCALE * (student_slope - (1.0 - BLEND) / members * probs)).astype(BF16)

    half = width // 2

    def term(which_core):
        chosen = jnp.take(places.reshape(chips, cores, cap), which_core, axis=1)
        result = 0.0
        for side in range(2):
            at = jnp.where(sides[None, :, None] == side, chosen[:, None, :], -1).reshape(-1, 1)
            unpack = (at == packed_ids[None, :]).astype(BF16)
            rows = jnp.dot(unpack, slope, preferred_element_type=F32).astype(BF16)
            result = result + lax.dot_general(
                rows,
                student_head[side * half : (side + 1) * half],
                (((1,), (1,)), ((), ())),
                preferred_element_type=F32,
            )
        return result

    arrived = lax.ppermute(term(1 - core), "core", swap)
    grads = ((term(core) + arrived) * GRAD_STEP).astype(F16).reshape(chips, 2 * cap, half)
    owned = jnp.sum(lax.all_to_all(grads, CHIPS, 0, 0, tiled=True).astype(F32), axis=0)
    slot_grad = jnp.concatenate([owned[:cap], owned[cap:]], axis=1) / GRAD_STEP
    live_here = slots < lax.dynamic_index_in_dim(counts, owner, keepdims=False)
    placed = (
        (jnp.arange(window, dtype=jnp.int32)[:, None] == slot_ids[None, :]) & live_here[None, :]
    ).astype(F32)
    hidden_grad = jnp.sum(placed[:, :, None] * slot_grad[None, :, :], axis=1).astype(BF16)
    return (mean_loss, hidden_grad)


def solution(mesh):
    fine = Mesh(mesh.devices.reshape(4, 8, 8, 2), ("member", "y", "z", "core"))
    placed = (
        P("member", OWNERS, None),
        P("member", None),
        P("member", None, OWNERS),
        P(OWNERS, "member"),
        P("member", OWNERS),
        P(OWNERS, None),
        P(),
        P(),
    )
    return jax.shard_map(
        on_device,
        mesh=fine,
        in_specs=placed,
        out_specs=(P(), P(OWNERS, "member")),
        check_vma=False,
    )
```
